32 devices in a mesh: ctx: 16 (over z, y, core), dp: 2 (over x).
Axes of the slice: x: 2, y: 2, z: 4, core: 2. Of those that a mesh axis runs over, the one named last changes fastest.
Arguments:
- features: bfloat16 [2, 3072, 1536], P('dp', 'ctx'), may hold values from -6 to 6
- bottleneck: bfloat16 [2, 3072, 384], P('dp', 'ctx'), may hold values from -6 to 6
- node_noise: bfloat16 [2, 3072, 1536], P('dp', 'ctx'), may hold values from -6 to 6
- targets: bfloat16 [2, 3072, 1536], P('dp', 'ctx'), may hold values from -15 to 15
- entry_weight: bfloat16 [384, 1536], P('ctx'), may hold values from -0.3125 to 0.3125
- conv_filters: bfloat16 [3, 1536, 384], P(None, None, 'ctx'), may hold values from -0.09375 to 0.09375
- exit_weight: bfloat16 [384, 1536], P('ctx'), may hold values from -0.3125 to 0.3125
Outputs:
- blended: bfloat16 [2, 3072, 1536], P('dp', 'ctx')
- estimate: float32 [384, 1536], P('ctx')
The draws below stay inside these ranges and needn't reach their ends.
All inputs are finite; a program needn't handle non-finite values.
Results may differ from the reference program's by a relative error of at most 0.015.
The reference program's roundings to bfloat16 on the way count: a program that leaves them out, or rounds other values in their place, can miss the bound.
Values may be sent and summed in bfloat16 or wider, within the bound.
A program may use at most 64 MiB of HBM per device.

```python
import jax
import jax.numpy as jnp
from jax import lax

CH = 1536
BOT = 384
DILATION = 32
BINS = 3072
SEQS = 2


def draw_targets(key, part):
    position = jnp.arange(BINS, dtype=jnp.float32)
    ramp = 0.5 + 4.5 * position / BINS
    values = jnp.clip(jax.random.normal(key, (SEQS, BINS, CH), jnp.float32), -3.0, 3.0)
    return (values * ramp[None, :, None]).astype(jnp.bfloat16)


def level_of(own_key, extent, shards, low, top_value):
    def one(axis_at, parts):
        heights = jax.random.uniform(jax.random.fold_in(jax.random.fold_in(own_key, 6), axis_at), (parts,), jnp.float32, low / len(shards), top_value / len(shards))
        return jnp.repeat(jnp.exp(heights), extent[axis_at] // parts).reshape((-1,) + (1,) * (len(extent) - axis_at - 1))

    level = one(*shards[0])
    for cut in shards[1:]:
        level = level * one(*cut)
    return level


def scatter_about(rng, dims, scale, limit, shards=(), held_as=jnp.bfloat16):
    factor_of = level_of(rng, dims, shards, -0.22, 0.18) if shards else 1.0
    drawn = jax.random.normal(rng, dims, jnp.float32) * scale * factor_of
    return jnp.minimum(jnp.maximum(drawn, -limit), limit).astype(held_as)


def setup_inputs(seed: int = 0) -> dict:
    seeds = jax.random.split(jax.random.key(seed), 8)
    features = scatter_about(seeds[0], (SEQS, BINS, CH), 1.0, 6.0, ((0, 2), (1, 16)))
    bottleneck = scatter_about(seeds[1], (SEQS, BINS, BOT), 1.0, 6.0, ((0, 2), (1, 16)))
    node_noise = scatter_about(seeds[2], (SEQS, BINS, CH), 1.0, 6.0, ((0, 2), (1, 16)))
    targets = draw_targets(jax.random.fold_in(seeds[7], 71), 0)
    entry_weight = scatter_about(seeds[4], (BOT, CH), BOT ** -0.5, 0.3125, ((0, 16),))
    conv_filters = scatter_about(seeds[5], (3, CH, BOT), (3 * CH) ** -0.5, 0.09375, ((2, 16),))
    exit_weight = scatter_about(seeds[6], (BOT, CH), BOT ** -0.5, 0.3125, ((0, 16),))
    return {"features": features, "bottleneck": bottleneck, "node_noise": node_noise, "targets": targets, "entry_weight": entry_weight, "conv_filters": conv_filters, "exit_weight": exit_weight}


NOISE_SCALE = 0.1


def second_block(state, conv_filters, exit_weight):
    activated = jax.nn.gelu(state).astype(jnp.bfloat16)
    padded = jnp.pad(activated, ((DILATION, DILATION), (0, 0)))
    length = state.shape[0]
    mixed = jnp.dot(padded[0:length], conv_filters[0], preferred_element_type=jnp.float32)
    mixed = mixed + jnp.dot(padded[DILATION:DILATION + length], conv_filters[1], preferred_element_type=jnp.float32)
    mixed = mixed + jnp.dot(padded[2 * DILATION:2 * DILATION + length], conv_filters[2], preferred_element_type=jnp.float32)
    inner = jax.nn.gelu(mixed).astype(jnp.bfloat16)
    return state + jnp.dot(inner, exit_weight, preferred_element_type=jnp.float32)


def reference(features, bottleneck, node_noise, targets, entry_weight, conv_filters, exit_weight):
    def one_sequence(items):
        feats, bottle, jitter, goal = items
        baseline = feats.astype(jnp.float32) + jnp.dot(bottle, entry_weight, preferred_element_type=jnp.float32)
        offset = jitter.astype(jnp.float32) * NOISE_SCALE
        upper = second_block(baseline + offset, conv_filters, exit_weight)
        lower = second_block(baseline - offset, conv_filters, exit_weight)
        blended = ((upper + lower) * 0.5).astype(jnp.bfloat16)
        gap = jnp.sum((upper - lower) * (upper + lower - 2.0 * goal.astype(jnp.float32))) / (BINS * CH)
        summed = lax.dot_general(bottle, jitter, (((0,), (0,)), ((), ())), preferred_element_type=jnp.float32)
        return blended, (gap / (2.0 * NOISE_SCALE)) * summed

    blended_all, weighted = lax.map(one_sequence, (features, bottleneck, node_noise, targets))
    return blended_all, jnp.sum(weighted, axis=0)
```

```python
import functools

import jax
import jax.numpy as jnp
from jax import lax
from jax.experimental import pallas as pl
from jax.experimental.pallas import tpu as pltpu
from jax.sharding import PartitionSpec as P

DILATION = 32


NOISE_SCALE = 0.1


def padded_2(cells, sides, width):
    for axis, dim in sides:
        count = lax.axis_size(axis)
        ends = count - 1
        head = lax.slice_in_dim(cells, 0, width, axis=dim)
        tail = lax.slice_in_dim(cells, cells.shape[dim] - width, cells.shape[dim], axis=dim)
        cells = jnp.concatenate(
            [
                lax.ppermute(tail, axis, [(i, (i + 1) % count) for i in range(ends)]),
                cells,
                lax.ppermute(head, axis, [((i + 1) % count, i) for i in range(ends)]),
            ],
            axis=dim,
        )
    return cells


def taps_for(padded, row_count, spacing, portion):
    summed = jnp.dot(padded[..., 0:row_count, :], portion[0], preferred_element_type=jnp.float32)
    summed = summed + jnp.dot(
        padded[..., spacing : spacing + row_count, :],
        portion[1],
        preferred_element_type=jnp.float32,
    )
    summed = summed + jnp.dot(
        padded[..., 2 * spacing : 2 * spacing + row_count, :],
        portion[2],
        preferred_element_type=jnp.float32,
    )
    return summed


def rows_for(left_side, portion):
    return jnp.dot(left_side, portion, preferred_element_type=jnp.float32)


def body(features, bottleneck, node_noise, targets, entry_weight, conv_filters, exit_weight):
    feats = features[0]
    bottle = bottleneck[0]
    jitter = node_noise[0]
    goal = targets[0].astype(jnp.float32)
    row_count = feats.shape[0]
    chan_count = feats.shape[1]
    spacing = DILATION
    baseline = feats.astype(jnp.float32) + rows_for(
        bottle, lax.all_gather(entry_weight, "ctx", axis=0, tiled=True)
    )
    offset_field = jitter.astype(jnp.float32) * NOISE_SCALE
    results = []
    for polarity in (1.0, -1.0):
        state = baseline + polarity * offset_field
        activated = jax.nn.gelu(state).astype(jnp.bfloat16)
        padded = padded_2(activated, (("ctx", 0),), spacing)
        mixed = taps_for(
            padded, row_count, spacing, lax.all_gather(conv_filters, "ctx", axis=2, tiled=True)
        )
        inner = jax.nn.gelu(mixed).astype(jnp.bfloat16)
        results.append(
            state + rows_for(inner, lax.all_gather(exit_weight, "ctx", axis=0, tiled=True))
        )
    upper = results[0]
    lower = results[1]
    blended = ((upper + lower) * 0.5).astype(jnp.bfloat16)[None]
    local_gap = jnp.sum((upper - lower) * (upper + lower - 2.0 * goal)) / (
        row_count * lax.axis_size("ctx") * chan_count
    )
    factor = lax.psum(local_gap, "ctx") / (2.0 * NOISE_SCALE)
    local_term = factor * lax.dot_general(
        bottle, jitter, (((0,), (0,)), ((), ())), preferred_element_type=jnp.float32
    )
    grouped = lax.psum(local_term, "dp")
    estimate = lax.psum_scatter(grouped, "ctx", scatter_dimension=0, tiled=True)
    return (blended, estimate)


F32 = jnp.float32
BF16 = jnp.bfloat16
GROUP = 256
PHASES = ((0, 1), (1, 3), (4, 1))
HOPS = ((4, 3), (3, 4))


def chip_at(position, chips):
    return jnp.where(position < chips // 2, 2 * position, 2 * (chips - 1 - position) + 1)


def kernel(
    chips,
    feats, bottle, noise, goal, wpad,
    blended, estimate,
    weights, wpeer, fx, nx, bx, act, base, inner,
    keep, csend, crecv, ysend, yrecv, zsend, zrecv, xsend, xrecv, pair, prow, gaps1, gaps2,
    ring_recv, x_recv, core_recv, bulk_send, init_send, init_recv, halo_send, halo_recv, rs_send, rs_recv,
):
    rows, chans = feats.shape
    bot = bottle.shape[1]
    unit = wpad.shape[2]
    half = chans // 2
    groups = chans // GROUP
    side = groups // 2
    zs = chips // 2
    others = chips - 1
    dp = lax.axis_index("dp")
    ctx = lax.axis_index("ctx")
    count = 2 * chips
    core = lax.rem(ctx, 2)
    chip = ctx // 2
    yy = lax.rem(chip, 2)
    zz = chip // 2
    par = lax.rem(dp, 2)
    mate = dp + 1 - 2 * par
    place = jnp.where(yy == 0, zz, chips - 1 - zz)

    def at(d, z, y, c):
        return {"dp": d, "ctx": (z * 2 + y) * 2 + c}

    def on_ring(p):
        return lax.rem(p + chips, chips)

    twin = at(dp, zz, yy, 1 - core)
    across = at(mate, zz, yy, core)
    near = [(i, j, k) for i in range(2) for j in range(2) for k in range(2) if i or j or k]

    def near_dev(i, j, k):
        return at(
            mate if i else dp,
            zz,
            1 - yy if j else yy,
            1 - core if k else core,
        )

    left = {"dp": dp, "ctx": lax.rem(ctx + count - 1, count)}
    right = {"dp": dp, "ctx": lax.rem(ctx + 1, count)}
    line = [at(dp, lax.rem(zz + d, zs), yy, core) for d in range(1, zs)]
    peers = [near_dev(*n) for n in near] + line + [left, right]

    barrier = pltpu.get_barrier_semaphore()
    for peer in peers:
        pl.semaphore_signal(barrier, inc=1, device_id=peer, device_id_type=pl.DeviceIdType.MESH)
    pl.semaphore_wait(barrier, len(peers))

    def remote(src, dst, ssem, rsem, dev):
        c = pltpu.make_async_remote_copy(
            src_ref=src, dst_ref=dst, send_sem=ssem, recv_sem=rsem,
            device_id=dev, device_id_type=pl.DeviceIdType.MESH,
        )
        return c

    def drain(ref, sem):
        pltpu.make_async_copy(ref, ref, sem).wait()

    mine = pl.ds(core * side, side)
    theirs = pl.ds((1 - core) * side, side)
    inits = []
    for n, (first, size) in enumerate(PHASES):
        inits.append(
            remote(
                wpad.at[theirs, pl.ds(first, size)], wpeer.at[theirs, pl.ds(first, size)],
                init_send.at[n], init_recv.at[n], twin,
            )
        )
    inits.append(remote(wpad.at[mine], wpeer.at[mine], init_send.at[3], init_recv.at[3], twin))
    for c in inits:
        c.start()
    halos = []
    for n, (src, dst) in enumerate(((feats, fx), (noise, nx), (bottle, bx))):
        w = DILATION
        halos.append(
            remote(src.at[pl.ds(0, w)], dst.at[pl.ds(w + rows, w)], halo_send.at[2 * n], halo_recv.at[2 * n], left)
        )
        halos.append(
            remote(src.at[pl.ds(rows - w, w)], dst.at[pl.ds(0, w)], halo_send.at[2 * n + 1], halo_recv.at[2 * n + 1], right)
        )
    for c in halos:
        c.start()

    own_rows = pl.ds(pl.multiple_of(chip * unit, 16), unit)
    g_ring = (core * side, core * side + 1 + par)
    g_x = core * side + 2 - par

    def piece(n, g, q):
        first, size = PHASES[n]
        return weights.at[g, pl.ds(first, size), pl.ds(pl.multiple_of(q * unit, 16), unit), :]

    def slot(n, j, d, h):
        return n * 2 * others + j * others + (h - 1 if d == 0 else HOPS[j][0] + h - 1)

    def origin(d, h):
        return chip_at(on_ring(place - h if d == 0 else place + h), chips)

    def toward(d):
        q = chip_at(on_ring(place + 1 if d == 0 else place - 1), chips)
        return {"dp": dp, "ctx": q * 2 + core}

    nexts = (toward(0), toward(1))

    def ring_copy(n, j, d, h):
        q = origin(d, h - 1)
        p = piece(n, g_ring[j], q)
        return remote(p, p, bulk_send.at[0], ring_recv.at[slot(n, j, d, h)], nexts[d])

    def ring_wait(n, j, d, h):
        p = piece(n, g_ring[j], origin(d, h))
        remote(p, p, bulk_send.at[0], ring_recv.at[slot(n, j, d, h)], nexts[d]).wait_recv()

    def to_twin(n, g, q):
        p = piece(n, g, q)
        remote(p, p, bulk_send.at[2], core_recv.at[n], twin).start()

    def hop(n, h):
        for j in range(2):
            for d in range(2):
                if h > HOPS[j][d]:
                    continue
                ring_wait(n, j, d, h)
                if h < HOPS[j][d]:
                    ring_copy(n, j, d, h + 1).start()
                q = origin(d, h)
                if j == 1:
                    p = piece(n, g_ring[1], q)
                    remote(p, p, bulk_send.at[1], x_recv.at[n * others + slot(0, 1, d, h) - others], across).start()
        for j in range(2):
            for d in range(2):
                if h <= HOPS[j][d]:
                    to_twin(n, g_ring[j], origin(d, h))

    def xhop(n, h):
        for d in range(2):
            if h > HOPS[1][d]:
                continue
            q = origin(d, h)
            p = piece(n, g_x, q)
            remote(p, p, bulk_send.at[1], x_recv.at[n * others + slot(0, 1, d, h) - others], across).wait_recv()
            to_twin(n, g_x, q)

    def settle(n):
        first, size = PHASES[n]
        drain(weights.at[pl.ds(0, side), pl.ds(first, size), pl.ds(0, others * unit)], core_recv.at[n])

    def assemble(n, begin):
        first, size = PHASES[n]
        for g in range(side):
            for m in range(first, first + size):
                weights[begin + g, m, own_rows, :] = wpad[begin + g, m] + wpeer[begin + g, m]

    def launch(n):
        p = remote(wpad.at[mine, pl.ds(*PHASES[n])], wpeer.at[mine, pl.ds(*PHASES[n])], init_send.at[n], init_recv.at[n], twin)
        p.wait_recv()
        assemble(n, core * side)
        for j in range(2):
            for d in range(2):
                ring_copy(n, j, d, 1).start()

    launch(0)
    launch(1)
    w = DILATION
    fx[w:w + rows, :] = feats[...]
    nx[w:w + rows, :] = noise[...]
    bx[w:w + rows, :] = bottle[...]
    hop(0, 1)

    def outer(g):
        cols = pl.ds(pl.multiple_of(g * GROUP, GROUP), GROUP)
        return lax.dot_general(bottle[...], noise[:, cols], (((0,), (0,)), ((), ())), preferred_element_type=F32)

    for g in range(side):
        csend[:, :, g * GROUP:(g + 1) * GROUP] = outer((1 - core) * side + g).astype(BF16).reshape(chips, unit, GROUP)
    rs_core = remote(csend, crecv, rs_send.at[0], rs_recv.at[0], twin)
    rs_core.start()
    hop(0, 2)
    launch(2)
    for g in range(side):
        keep[:, :, g * GROUP:(g + 1) * GROUP] = outer(core * side + g).reshape(chips, unit, GROUP)
    hop(0, 3)
    xhop(0, 1)
    rs_core.wait_recv()
    for z in range(zs):
        ysend[z] = (keep[2 * z + 1 - yy] + crecv[2 * z + 1 - yy].astype(F32)).astype(BF16)
    rs_y = remote(ysend, yrecv, rs_send.at[1], rs_recv.at[1], near_dev(0, 1, 0))
    rs_y.start()
    hop(0, 4)
    xhop(0, 2)
    hop(1, 1)
    xhop(0, 3)
    xhop(0, 4)
    remote(wpad.at[theirs], wpeer.at[theirs], init_send.at[3], init_recv.at[3], twin).wait_recv()
    for n in range(3):
        assemble(n, (1 - core) * side)
    for c in halos:
        c.wait()
    rs_y.wait_recv()
    for z in range(zs):
        total = keep[2 * z + yy] + crecv[2 * z + yy].astype(F32) + yrecv[z].astype(F32)
        keep[2 * z + yy] = total
        zsend[z] = total.astype(BF16)
    rs_z = []
    for d in range(1, zs):
        c = remote(zsend.at[lax.rem(zz + d, zs)], zrecv.at[d - 1], rs_send.at[1 + d], rs_recv.at[1 + d], line[d - 1])
        c.start()
        rs_z.append(c)
    settle(0)

    edge = lax.broadcasted_iota(jnp.int32, (rows + 2 * w, 1), 0)
    inside = jnp.logical_and(
        jnp.logical_or(edge >= w, ctx > 0), jnp.logical_or(edge < w + rows, ctx < count - 1)
    )

    def enter(g):
        cols = pl.ds(g * GROUP, GROUP)
        b = fx[:, cols].astype(F32) + jnp.dot(bx[...], weights[g, 0], preferred_element_type=F32)
        off = nx[:, cols].astype(F32) * NOISE_SCALE
        base[:, cols] = b[w:w + rows]
        for p, state in enumerate((b + off, b - off)):
            act[p, :, cols] = jnp.where(inside, jax.nn.gelu(state), 0.0).astype(BF16)

    enter(0)
    enter(1)
    hop(1, 2)
    xhop(1, 1)
    enter(2)
    enter(3)
    hop(1, 3)
    xhop(1, 2)
    enter(4)
    enter(5)
    hop(1, 4)
    xhop(1, 3)
    hop(2, 1)
    xhop(1, 4)
    hop(2, 2)
    xhop(2, 1)
    for c in rs_z:
        c.wait_recv()
    owned = keep[chip]
    for d in range(zs - 1):
        owned = owned + zrecv[d].astype(F32)
    pair[par] = owned
    xsend[...] = owned.astype(BF16)
    rs_x = remote(xsend, xrecv, rs_send.at[1 + zs], rs_recv.at[1 + zs], across)
    rs_x.start()
    settle(1)

    def mix(k, p):
        total = jnp.zeros((rows, bot), F32)
        for g in range(groups):
            total = total + lax.dot_general(
                act[p, k * w:k * w + rows, g * GROUP:(g + 1) * GROUP], weights[g, 1 + k],
                (((1,), (1,)), ((), ())), preferred_element_type=F32,
            )
        return total

    def mixed(p):
        inner[p] = jax.nn.gelu(mix(0, p) + mix(1, p) + mix(2, p)).astype(BF16)

    mixed(0)
    hop(2, 3)
    xhop(2, 2)
    mixed(1)
    hop(2, 4)
    xhop(2, 3)
    xhop(2, 4)
    rs_x.wait_recv()
    pair[1 - par] = xrecv[...].astype(F32)
    give = pl.ds(pl.multiple_of((1 - core) * (unit // 2), 8), unit // 2)
    have = pl.ds(pl.multiple_of(core * (unit // 2), 8), unit // 2)
    rs_f = remote(pair.at[:, give, :], prow, rs_send.at[2 + zs], rs_recv.at[2 + zs], twin)
    rs_f.start()
    settle(2)

    lanes = jnp.zeros((1, GROUP), F32)
    for g in range(groups):
        cols = pl.ds(g * GROUP, GROUP)
        off = noise[:, cols].astype(F32) * NOISE_SCALE
        b = base[:, cols]
        upper = b + off + jnp.dot(inner[0], weights[g, 4], preferred_element_type=F32)
        lower = b - off + jnp.dot(inner[1], weights[g, 4], preferred_element_type=F32)
        both = upper + lower
        blended[:, cols] = (both * 0.5).astype(BF16)
        lanes = lanes + jnp.sum((upper - lower) * (both - 2.0 * goal[:, cols].astype(F32)), axis=0, keepdims=True)
    local = jnp.sum(lanes, axis=1, keepdims=True) / (rows * count * chans)
    shelf = lax.broadcasted_iota(jnp.int32, (8, 128), 0)
    gaps1[0] = jnp.where(shelf == par, local, 0.0)
    sent = []
    for i, n in enumerate(near):
        c = remote(gaps1.at[0], gaps1.at[i + 1], bulk_send.at[3], bulk_send.at[4], near_dev(*n))
        c.start()
    drain(gaps1.at[pl.ds(1, len(near))], bulk_send.at[4])
    drain(gaps1.at[pl.ds(1, len(near))], bulk_send.at[3])
    gaps2[0] = jnp.sum(gaps1[...], axis=0)
    for d in range(1, zs):
        remote(gaps2.at[0], gaps2.at[d], bulk_send.at[5], bulk_send.at[6], line[d - 1]).start()
    rs_f.wait()
    drain(gaps2.at[pl.ds(1, zs - 1)], bulk_send.at[6])
    drain(gaps2.at[pl.ds(1, zs - 1)], bulk_send.at[5])
    factors = jnp.sum(gaps2[...], axis=0) / (2.0 * NOISE_SCALE)
    f0 = factors[0:1, 0:1]
    f1 = factors[1:2, 0:1]
    here = pl.ds(pl.multiple_of(core * half, 128), half)
    there = pl.ds(pl.multiple_of((1 - core) * half, 128), half)
    estimate[:, here] = f0 * pair[0, have, :] + f1 * pair[1, have, :]
    estimate[:, there] = f0 * prow[0] + f1 * prow[1]

    rs_core.wait_send()
    rs_y.wait_send()
    rs_x.wait_send()
    for c in rs_z:
        c.wait_send()
    for c in inits:
        c.wait_send()
    for n, ways in enumerate((2, 1, 3)):
        drain(weights.at[pl.ds(0, ways), :, pl.ds(0, others * unit)], bulk_send.at[n])


def fused(features, bottleneck, node_noise, targets, entry_weight, conv_filters, exit_weight):
    count = lax.axis_size("ctx")
    chips = count // 2
    _, rows, chans = features.shape
    bot = bottleneck.shape[2]
    share = entry_weight.shape[0]
    unit = 2 * share
    groups = chans // GROUP
    zs = chips // 2
    core = lax.axis_index("ctx") % 2
    shard = jnp.concatenate([entry_weight[None], jnp.swapaxes(conv_filters, 1, 2), exit_weight[None]], axis=0)
    shard = shard.reshape(5, share, groups, GROUP).transpose(2, 0, 1, 3)
    none = jnp.zeros_like(shard)
    wpad = jnp.concatenate(
        [jnp.where(core == 0, shard, none), jnp.where(core == 1, shard, none)], axis=2
    )
    wide = rows + 2 * DILATION
    half = chans // 2
    blended, estimate = pl.pallas_call(
        functools.partial(kernel, chips),
        out_shape=(
            jax.ShapeDtypeStruct((rows, chans), BF16),
            jax.ShapeDtypeStruct((share, chans), F32),
        ),
        in_specs=[pl.BlockSpec(memory_space=pltpu.VMEM)] * 5,
        out_specs=[pl.BlockSpec(memory_space=pltpu.VMEM)] * 2,
        scratch_shapes=[
            pltpu.VMEM((groups, 5, bot, GROUP), BF16),
            pltpu.VMEM((groups, 5, unit, GROUP), BF16),
            pltpu.VMEM((wide, chans), BF16),
            pltpu.VMEM((wide, chans), BF16),
            pltpu.VMEM((wide, bot), BF16),
            pltpu.VMEM((2, wide, chans), BF16),
            pltpu.VMEM((rows, chans), F32),
            pltpu.VMEM((2, rows, bot), BF16),
            pltpu.VMEM((chips, unit, half), F32),
            pltpu.VMEM((chips, unit, half), BF16),
            pltpu.VMEM((chips, unit, half), BF16),
            pltpu.VMEM((zs, unit, half), BF16),
            pltpu.VMEM((zs, unit, half), BF16),
            pltpu.VMEM((zs, unit, half), BF16),
            pltpu.VMEM((zs - 1, unit, half), BF16),
            pltpu.VMEM((unit, half), BF16),
            pltpu.VMEM((unit, half), BF16),
            pltpu.VMEM((2, unit, half), F32),
            pltpu.VMEM((2, unit // 2, half), F32),
            pltpu.VMEM((8, 8, 128), F32),
            pltpu.VMEM((zs, 8, 128), F32),
            pltpu.SemaphoreType.DMA((3 * 2 * (chips - 1),)),
            pltpu.SemaphoreType.DMA((3 * (chips - 1),)),
            pltpu.SemaphoreType.DMA((3,)),
            pltpu.SemaphoreType.DMA((7,)),
            pltpu.SemaphoreType.DMA((4,)),
            pltpu.SemaphoreType.DMA((4,)),
            pltpu.SemaphoreType.DMA((6,)),
            pltpu.SemaphoreType.DMA((6,)),
            pltpu.SemaphoreType.DMA((3 + zs,)),
            pltpu.SemaphoreType.DMA((3 + zs,)),
        ],
        compiler_params=pltpu.CompilerParams(
            collective_id=0, has_side_effects=True, vmem_limit_bytes=48 * 1024 * 1024
        ),
    )(features[0], bottleneck[0], node_noise[0], targets[0], wpad)
    return blended[None], estimate


def solution(mesh):
    small = mesh.shape["ctx"] == 16 and mesh.shape["dp"] == 2
    return jax.shard_map(
        fused if small else body,
        mesh=mesh,
        in_specs=(
            P("dp", "ctx", None),
            P("dp", "ctx", None),
            P("dp", "ctx", None),
            P("dp", "ctx", None),
            P("ctx", None),
            P(None, None, "ctx"),
            P("ctx", None),
        ),
        out_specs=(P("dp", "ctx", None), P("ctx", None)),
        check_vma=False,
    )
```

```python
import functools

import jax
import jax.numpy as jnp
from jax import lax
from jax.experimental import pallas as pl
from jax.experimental.pallas import tpu as pltpu
from jax.sharding import PartitionSpec as P

DILATION = 32


NOISE_SCALE = 0.1


def padded_2(cells, sides, width):
    for axis, dim in sides:
        count = lax.axis_size(axis)
        ends = count - 1
        head = lax.slice_in_dim(cells, 0, width, axis=dim)
        tail = lax.slice_in_dim(cells, cells.shape[dim] - width, cells.shape[dim], axis=dim)
        cells = jnp.concatenate(
            [
                lax.ppermute(tail, axis, [(i, (i + 1) % count) for i in range(ends)]),
                cells,
                lax.ppermute(head, axis, [((i + 1) % count, i) for i in range(ends)]),
            ],
            axis=dim,
        )
    return cells


def taps_for(padded, row_count, spacing, portion):
    summed = jnp.dot(padded[..., 0:row_count, :], portion[0], preferred_element_type=jnp.float32)
    summed = summed + jnp.dot(
        padded[..., spacing : spacing + row_count, :],
        portion[1],
        preferred_element_type=jnp.float32,
    )
    summed = summed + jnp.dot(
        padded[..., 2 * spacing : 2 * spacing + row_count, :],
        portion[2],
        preferred_element_type=jnp.float32,
    )
    return summed


def rows_for(left_side, portion):
    return jnp.dot(left_side, portion, preferred_element_type=jnp.float32)


def body(features, bottleneck, node_noise, targets, entry_weight, conv_filters, exit_weight):
    feats = features[0]
    bottle = bottleneck[0]
    jitter = node_noise[0]
    goal = targets[0].astype(jnp.float32)
    row_count = feats.shape[0]
    chan_count = feats.shape[1]
    spacing = DILATION
    baseline = feats.astype(jnp.float32) + rows_for(
        bottle, lax.all_gather(entry_weight, "ctx", axis=0, tiled=True)
    )
    offset_field = jitter.astype(jnp.float32) * NOISE_SCALE
    results = []
    for polarity in (1.0, -1.0):
        state = baseline + polarity * offset_field
        activated = jax.nn.gelu(state).astype(jnp.bfloat16)
        padded = padded_2(activated, (("ctx", 0),), spacing)
        mixed = taps_for(
            padded, row_count, spacing, lax.all_gather(conv_filters, "ctx", axis=2, tiled=True)
        )
        inner = jax.nn.gelu(mixed).astype(jnp.bfloat16)
        results.append(
            state + rows_for(inner, lax.all_gather(exit_weight, "ctx", axis=0, tiled=True))
        )
    upper = results[0]
    lower = results[1]
    blended = ((upper + lower) * 0.5).astype(jnp.bfloat16)[None]
    local_gap = jnp.sum((upper - lower) * (upper + lower - 2.0 * goal)) / (
        row_count * lax.axis_size("ctx") * chan_count
    )
    factor = lax.psum(local_gap, "ctx") / (2.0 * NOISE_SCALE)
    local_term = factor * lax.dot_general(
        bottle, jitter, (((0,), (0,)), ((), ())), preferred_element_type=jnp.float32
    )
    grouped = lax.psum(local_term, "dp")
    estimate = lax.psum_scatter(grouped, "ctx", scatter_dimension=0, tiled=True)
    return (blended, estimate)


F32 = jnp.float32
BF16 = jnp.bfloat16
GROUP = 256
PHASES = ((0, 1), (1, 3), (4, 1))
HOPS = 4


def chip_at(position, chips):
    return jnp.where(position < chips // 2, 2 * position, 2 * (chips - 1 - position) + 1)


def kernel(
    chips,
    feats, bottle, noise, goal, entry, filters, leave,
    blended, estimate,
    weights, wpad, wpeer, fx, nx, bx, gx, act, base, mixed, inner,
    keep, csend, crecv, ysend, yrecv, zsend, zrecv, xsend, xrecv, pair, prow, gaps1, gaps2,
    ring_recv, x_recv, core_recv, bulk_send, init_send, init_recv, halo_send, halo_recv, rs_send, rs_recv, load,
):
    rows, chans = feats.shape
    bot = bottle.shape[1]
    share = entry.shape[0]
    unit = 2 * share
    half = chans // 2
    groups = chans // GROUP
    side = groups // 2
    zs = chips // 2
    others = chips - 1
    dp = lax.axis_index("dp")
    ctx = lax.axis_index("ctx")
    count = 2 * chips
    core = lax.rem(ctx, 2)
    chip = ctx // 2
    yy = lax.rem(chip, 2)
    zz = chip // 2
    par = lax.rem(dp, 2)
    mate = dp + 1 - 2 * par
    place = jnp.where(yy == 0, zz, chips - 1 - zz)

    def at(d, z, y, c):
        return {"dp": d, "ctx": (z * 2 + y) * 2 + c}

    def on_ring(p):
        return lax.rem(p + chips, chips)

    twin = at(dp, zz, yy, 1 - core)
    across = at(mate, zz, yy, core)
    near = [(i, j, k) for i in range(2) for j in range(2) for k in range(2) if i or j or k]

    def near_dev(i, j, k):
        return at(
            mate if i else dp,
            zz,
            1 - yy if j else yy,
            1 - core if k else core,
        )

    left = {"dp": dp, "ctx": lax.rem(ctx + count - 1, count)}
    right = {"dp": dp, "ctx": lax.rem(ctx + 1, count)}
    line = [at(dp, lax.rem(zz + d, zs), yy, core) for d in range(1, zs)]
    peers = [near_dev(*n) for n in near] + line + [left, right]

    w = DILATION
    middle = pl.ds(w, rows)
    loads = [
        pltpu.make_async_copy(src, dst, load.at[n])
        for n, (src, dst) in enumerate(
            (
                (bottle, bx.at[middle]), (noise, nx.at[middle]), (feats, fx.at[middle]), (goal, gx),
            )
        )
    ]
    for c in loads:
        c.start()
    blank = jnp.zeros((share, GROUP), F32)
    for g in range(groups):
        for m in range(5):
            shard = entry if m == 0 else leave if m == 4 else filters.at[m - 1]
            part = shard[:, g * GROUP:(g + 1) * GROUP].astype(F32)
            low = jnp.concatenate([part, blank], axis=0)
            high = jnp.concatenate([blank, part], axis=0)
            wpad[g, m] = jnp.where(core == 0, low, high).astype(BF16)

    barrier = pltpu.get_barrier_semaphore()
    for peer in peers:
        pl.semaphore_signal(barrier, inc=1, device_id=peer, device_id_type=pl.DeviceIdType.MESH)
    pl.semaphore_wait(barrier, len(peers))

    def remote(src, dst, ssem, rsem, dev):
        c = pltpu.make_async_remote_copy(
            src_ref=src, dst_ref=dst, send_sem=ssem, recv_sem=rsem,
            device_id=dev, device_id_type=pl.DeviceIdType.MESH,
        )
        return c

    def drain(ref, sem):
        pltpu.make_async_copy(ref, ref, sem).wait()

    mine = pl.ds(core * side, side)
    theirs = pl.ds((1 - core) * side, side)
    inits = []
    for n, (first, size) in enumerate(PHASES):
        inits.append(
            remote(
                wpad.at[theirs, pl.ds(first, size)], wpeer.at[theirs, pl.ds(first, size)],
                init_send.at[n], init_recv.at[n], twin,
            )
        )
    inits.append(remote(wpad.at[mine], wpeer.at[mine], init_send.at[3], init_recv.at[3], twin))
    for c in inits:
        c.start()
    halos = []
    for n, (src, dst) in enumerate(((feats, fx), (noise, nx), (bottle, bx))):
        halos.append(
            remote(src.at[pl.ds(0, w)], dst.at[pl.ds(w + rows, w)], halo_send.at[2 * n], halo_recv.at[2 * n], left)
        )
        halos.append(
            remote(src.at[pl.ds(rows - w, w)], dst.at[pl.ds(0, w)], halo_send.at[2 * n + 1], halo_recv.at[2 * n + 1], right)
        )
    for c in halos:
        c.start()

    own_rows = pl.ds(pl.multiple_of(chip * unit, 16), unit)
    spans = {
        (d, h): pl.ds(
            pl.multiple_of(chip_at(on_ring(place - h if d == 0 else place + h), chips) * unit, 16), unit
        )
        for d in range(2)
        for h in range(HOPS + 1)
    }
    g_pair = core * side + par
    g_mid = core * side + 1
    g_own = core * side + 2 * par
    g_x = core * side + 2 - 2 * par

    def piece(n, g, many, d, h):
        first, size = PHASES[n]
        return weights.at[pl.ds(g, many), pl.ds(first, size), spans[d, h], :]

    def ring_piece(n, d, h, start):
        if h < HOPS:
            return piece(n, g_pair, 2, d, start)
        return piece(n, g_mid if d == 0 else g_own, 1, d, start)

    def toward(d):
        q = chip_at(on_ring(place + 1 if d == 0 else place - 1), chips)
        return {"dp": dp, "ctx": q * 2 + core}

    nexts = (toward(0), toward(1))

    def ring_copy(n, d, h, start):
        p = ring_piece(n, d, h, start)
        return remote(p, p, bulk_send.at[0], ring_recv.at[n * 2 * HOPS + 2 * (h - 1) + d], nexts[d])

    def to_twin(n, p):
        remote(p, p, bulk_send.at[2], core_recv.at[n], twin).start()

    def x_copy(n, d, h, g):
        p = piece(n, g, 1, d, h)
        return remote(p, p, bulk_send.at[1], x_recv.at[n * 2 * HOPS + 2 * (h - 1) + d], across)

    def hop(n, h):
        for d in range(2):
            ring_copy(n, d, h, h).wait_recv()
            if h < HOPS:
                ring_copy(n, d, h + 1, h).start()
            if h < HOPS or d == 1:
                x_copy(n, d, h, g_own).start()
        for d in range(2):
            to_twin(n, ring_piece(n, d, h, h))

    def xhop(n, h):
        for d in range(2):
            if h < HOPS or d == 1:
                x_copy(n, d, h, g_x).wait_recv()
                to_twin(n, piece(n, g_x, 1, d, h))

    def settle(n):
        first, size = PHASES[n]
        drain(weights.at[pl.ds(0, side), pl.ds(first, size), pl.ds(0, others * unit)], core_recv.at[n])

    def assemble(n, begin):
        first, size = PHASES[n]
        for g in range(side):
            for m in range(first, first + size):
                weights[begin + g, m, own_rows, :] = wpad[begin + g, m] + wpeer[begin + g, m]

    def launch(n):
        p = remote(wpad.at[mine, pl.ds(*PHASES[n])], wpeer.at[mine, pl.ds(*PHASES[n])], init_send.at[n], init_recv.at[n], twin)
        p.wait_recv()
        assemble(n, core * side)
        for d in range(2):
            ring_copy(n, d, 1, 0).start()

    launch(0)
    launch(1)
    for c in loads:
        c.wait()

    def outer(g):
        cols = pl.ds(pl.multiple_of(g * GROUP, GROUP), GROUP)
        return lax.dot_general(
            bx[middle, :], nx[middle, cols], (((0,), (0,)), ((), ())), preferred_element_type=F32
        ).reshape(chips, unit, GROUP)

    for g in range(side):
        csend[:, :, g * GROUP:(g + 1) * GROUP] = outer((1 - core) * side + g).astype(BF16)
    rs_core = remote(csend, crecv, rs_send.at[0], rs_recv.at[0], twin)
    rs_core.start()
    hop(0, 1)
    launch(2)
    for g in range(side):
        keep[:, :, g * GROUP:(g + 1) * GROUP] = outer(core * side + g)
    hop(0, 2)
    xhop(0, 1)
    hop(1, 1)
    rs_core.wait_recv()
    for z in range(zs):
        ysend[z] = (keep[2 * z + 1 - yy] + crecv[2 * z + 1 - yy].astype(F32)).astype(BF16)
    rs_y = remote(ysend, yrecv, rs_send.at[1], rs_recv.at[1], near_dev(0, 1, 0))
    rs_y.start()
    hop(0, 3)
    xhop(0, 2)
    remote(wpad.at[theirs], wpeer.at[theirs], init_send.at[3], init_recv.at[3], twin).wait_recv()
    for n in range(3):
        assemble(n, (1 - core) * side)
    hop(0, 4)
    xhop(0, 3)
    hop(1, 2)
    xhop(0, 4)
    xhop(1, 1)
    hop(2, 1)
    rs_y.wait_recv()
    for z in range(zs):
        total = keep[2 * z + yy] + crecv[2 * z + yy].astype(F32) + yrecv[z].astype(F32)
        keep[2 * z + yy] = total
        zsend[z] = total.astype(BF16)
    rs_z = []
    for d in range(1, zs):
        c = remote(zsend.at[lax.rem(zz + d, zs)], zrecv.at[d - 1], rs_send.at[1 + d], rs_recv.at[1 + d], line[d - 1])
        c.start()
        rs_z.append(c)
    for c in halos:
        c.wait()
    settle(0)

    edge = lax.broadcasted_iota(jnp.int32, (rows + 2 * w, 1), 0)
    inside = jnp.logical_and(
        jnp.logical_or(edge >= w, ctx > 0), jnp.logical_or(edge < w + rows, ctx < count - 1)
    )

    def enter(g):
        cols = pl.ds(g * GROUP, GROUP)
        b = fx[:, cols].astype(F32) + jnp.dot(bx[...], weights[g, 0], preferred_element_type=F32)
        off = nx[:, cols].astype(F32) * NOISE_SCALE
        base[:, cols] = b[w:w + rows]
        for p, state in enumerate((b + off, b - off)):
            act[p, :, cols] = jnp.where(inside, jax.nn.gelu(state), 0.0).astype(BF16)

    enter(0)
    hop(1, 3)
    xhop(1, 2)
    enter(1)
    hop(2, 2)
    xhop(2, 1)
    enter(2)
    hop(1, 4)
    xhop(1, 3)
    enter(3)
    hop(2, 3)
    xhop(1, 4)
    xhop(2, 2)
    enter(4)
    enter(5)
    for c in rs_z:
        c.wait_recv()
    owned = keep[chip]
    for d in range(zs - 1):
        owned = owned + zrecv[d].astype(F32)
    pair[par] = owned
    xsend[...] = owned.astype(BF16)
    rs_x = remote(xsend, xrecv, rs_send.at[1 + zs], rs_recv.at[1 + zs], across)
    rs_x.start()
    settle(1)

    def mix(k):
        total = jnp.zeros((2 * rows, bot), F32)
        for g in range(groups):
            left_side = act[:, k * w:k * w + rows, g * GROUP:(g + 1) * GROUP].reshape(2 * rows, GROUP)
            total = total + lax.dot_general(
                left_side, weights[g, 1 + k], (((1,), (1,)), ((), ())), preferred_element_type=F32
            )
        return total

    mixed[...] = mix(0)
    hop(2, 4)
    xhop(2, 3)
    mixed[...] += mix(1)
    xhop(2, 4)
    inner[...] = jax.nn.gelu(mixed[...] + mix(2)).astype(BF16)
    rs_x.wait_recv()
    pair[1 - par] = xrecv[...].astype(F32)
    give = pl.ds(pl.multiple_of((1 - core) * (unit // 2), 8), unit // 2)
    have = pl.ds(pl.multiple_of(core * (unit // 2), 8), unit // 2)
    rs_f = remote(pair.at[:, give, :], prow, rs_send.at[2 + zs], rs_recv.at[2 + zs], twin)
    rs_f.start()
    settle(2)

    lanes = jnp.zeros((1, GROUP), F32)
    for g in range(groups):
        cols = pl.ds(g * GROUP, GROUP)
        off = nx[middle, cols].astype(F32) * NOISE_SCALE
        b = base[:, cols]
        outs = jnp.dot(inner[...], weights[g, 4], preferred_element_type=F32)
        upper = b + off + outs[:rows]
        lower = b - off + outs[rows:]
        both = upper + lower
        blended[:, cols] = (both * 0.5).astype(BF16)
        lanes = lanes + jnp.sum((upper - lower) * (both - 2.0 * gx[:, cols].astype(F32)), axis=0, keepdims=True)
    local = jnp.sum(lanes, axis=1, keepdims=True) / (rows * count * chans)
    shelf = lax.broadcasted_iota(jnp.int32, (8, 128), 0)
    gaps1[0] = jnp.where(shelf == par, local, 0.0)
    sent = []
    for i, n in enumerate(near):
        c = remote(gaps1.at[0], gaps1.at[i + 1], bulk_send.at[3], bulk_send.at[4], near_dev(*n))
        c.start()
    drain(gaps1.at[pl.ds(1, len(near))], bulk_send.at[4])
    drain(gaps1.at[pl.ds(1, len(near))], bulk_send.at[3])
    gaps2[0] = jnp.sum(gaps1[...], axis=0)
    for d in range(1, zs):
        remote(gaps2.at[0], gaps2.at[d], bulk_send.at[5], bulk_send.at[6], line[d - 1]).start()
    rs_f.wait()
    drain(gaps2.at[pl.ds(1, zs - 1)], bulk_send.at[6])
    drain(gaps2.at[pl.ds(1, zs - 1)], bulk_send.at[5])
    factors = jnp.sum(gaps2[...], axis=0) / (2.0 * NOISE_SCALE)
    f0 = factors[0:1, 0:1]
    f1 = factors[1:2, 0:1]
    here = pl.ds(pl.multiple_of(core * half, 128), half)
    there = pl.ds(pl.multiple_of((1 - core) * half, 128), half)
    estimate[:, here] = f0 * pair[0, have, :] + f1 * pair[1, have, :]
    estimate[:, there] = f0 * prow[0] + f1 * prow[1]

    rs_core.wait_send()
    rs_y.wait_send()
    rs_x.wait_send()
    for c in rs_z:
        c.wait_send()
    for c in inits:
        c.wait_send()
    for n, ways in enumerate((2, 1, 3)):
        drain(weights.at[pl.ds(0, ways), :, pl.ds(0, others * unit)], bulk_send.at[n])


def fused(features, bottleneck, node_noise, targets, entry_weight, conv_filters, exit_weight):
    count = lax.axis_size("ctx")
    chips = count // 2
    _, rows, chans = features.shape
    bot = bottleneck.shape[2]
    share = entry_weight.shape[0]
    unit = 2 * share
    groups = chans // GROUP
    zs = chips // 2
    wide = rows + 2 * DILATION
    half = chans // 2
    blended, estimate = pl.pallas_call(
        functools.partial(kernel, chips),
        out_shape=(
            jax.ShapeDtypeStruct((rows, chans), BF16),
            jax.ShapeDtypeStruct((share, chans), F32),
        ),
        in_specs=[pl.BlockSpec(memory_space=pl.ANY)] * 4 + [pl.BlockSpec(memory_space=pltpu.VMEM)] * 3,
        out_specs=[pl.BlockSpec(memory_space=pltpu.VMEM)] * 2,
        scratch_shapes=[
            pltpu.VMEM((groups, 5, bot, GROUP), BF16),
            pltpu.VMEM((groups, 5, unit, GROUP), BF16),
            pltpu.VMEM((groups, 5, unit, GROUP), BF16),
            pltpu.VMEM((wide, chans), BF16),
            pltpu.VMEM((wide, chans), BF16),
            pltpu.VMEM((wide, bot), BF16),
            pltpu.VMEM((rows, chans), BF16),
            pltpu.VMEM((2, wide, chans), BF16),
            pltpu.VMEM((rows, chans), F32),
            pltpu.VMEM((2 * rows, bot), F32),
            pltpu.VMEM((2 * rows, bot), BF16),
            pltpu.VMEM((chips, unit, half), F32),
            pltpu.VMEM((chips, unit, half), BF16),
            pltpu.VMEM((chips, unit, half), BF16),
            pltpu.VMEM((zs, unit, half), BF16),
            pltpu.VMEM((zs, unit, half), BF16),
            pltpu.VMEM((zs, unit, half), BF16),
            pltpu.VMEM((zs - 1, unit, half), BF16),
            pltpu.VMEM((unit, half), BF16),
            pltpu.VMEM((unit, half), BF16),
            pltpu.VMEM((2, unit, half), F32),
            pltpu.VMEM((2, unit // 2, half), F32),
            pltpu.VMEM((8, 8, 128), F32),
            pltpu.VMEM((zs, 8, 128), F32),
            pltpu.SemaphoreType.DMA((3 * 2 * HOPS,)),
            pltpu.SemaphoreType.DMA((3 * 2 * HOPS,)),
            pltpu.SemaphoreType.DMA((3,)),
            pltpu.SemaphoreType.DMA((7,)),
            pltpu.SemaphoreType.DMA((4,)),
            pltpu.SemaphoreType.DMA((4,)),
            pltpu.SemaphoreType.DMA((6,)),
            pltpu.SemaphoreType.DMA((6,)),
            pltpu.SemaphoreType.DMA((3 + zs,)),
            pltpu.SemaphoreType.DMA((3 + zs,)),
            pltpu.SemaphoreType.DMA((4,)),
        ],
        compiler_params=pltpu.CompilerParams(
            collective_id=0, has_side_effects=True, vmem_limit_bytes=60 * 1024 * 1024
        ),
    )(
        features[0], bottleneck[0], node_noise[0], targets[0],
        entry_weight, jnp.swapaxes(conv_filters, 1, 2), exit_weight,
    )
    return blended[None], estimate


def solution(mesh):
    small = mesh.shape["ctx"] == 16 and mesh.shape["dp"] == 2
    return jax.shard_map(
        fused if small else body,
        mesh=mesh,
        in_specs=(
            P("dp", "ctx", None),
            P("dp", "ctx", None),
            P("dp", "ctx", None),
            P("dp", "ctx", None),
            P("ctx", None),
            P(None, None, "ctx"),
            P("ctx", None),
        ),
        out_specs=(P("dp", "ctx", None), P("ctx", None)),
        check_vma=False,
    )
```

```python
import functools

import jax
import jax.numpy as jnp
from jax import lax
from jax.experimental import pallas as pl
from jax.experimental.pallas import tpu as pltpu
from jax.sharding import PartitionSpec as P

DILATION = 32


NOISE_SCALE = 0.1


def padded_2(cells, sides, width):
    for axis, dim in sides:
        count = lax.axis_size(axis)
        ends = count - 1
        head = lax.slice_in_dim(cells, 0, width, axis=dim)
        tail = lax.slice_in_dim(cells, cells.shape[dim] - width, cells.shape[dim], axis=dim)
        cells = jnp.concatenate(
            [
                lax.ppermute(tail, axis, [(i, (i + 1) % count) for i in range(ends)]),
                cells,
                lax.ppermute(head, axis, [((i + 1) % count, i) for i in range(ends)]),
            ],
            axis=dim,
        )
    return cells


def taps_for(padded, row_count, spacing, portion):
    summed = jnp.dot(padded[..., 0:row_count, :], portion[0], preferred_element_type=jnp.float32)
    summed = summed + jnp.dot(
        padded[..., spacing : spacing + row_count, :],
        portion[1],
        preferred_element_type=jnp.float32,
    )
    summed = summed + jnp.dot(
        padded[..., 2 * spacing : 2 * spacing + row_count, :],
        portion[2],
        preferred_element_type=jnp.float32,
    )
    return summed


def rows_for(left_side, portion):
    return jnp.dot(left_side, portion, preferred_element_type=jnp.float32)


def body(features, bottleneck, node_noise, targets, entry_weight, conv_filters, exit_weight):
    feats = features[0]
    bottle = bottleneck[0]
    jitter = node_noise[0]
    goal = targets[0].astype(jnp.float32)
    row_count = feats.shape[0]
    chan_count = feats.shape[1]
    spacing = DILATION
    baseline = feats.astype(jnp.float32) + rows_for(
        bottle, lax.all_gather(entry_weight, "ctx", axis=0, tiled=True)
    )
    offset_field = jitter.astype(jnp.float32) * NOISE_SCALE
    results = []
    for polarity in (1.0, -1.0):
        state = baseline + polarity * offset_field
        activated = jax.nn.gelu(state).astype(jnp.bfloat16)
        padded = padded_2(activated, (("ctx", 0),), spacing)
        mixed = taps_for(
            padded, row_count, spacing, lax.all_gather(conv_filters, "ctx", axis=2, tiled=True)
        )
        inner = jax.nn.gelu(mixed).astype(jnp.bfloat16)
        results.append(
            state + rows_for(inner, lax.all_gather(exit_weight, "ctx", axis=0, tiled=True))
        )
    upper = results[0]
    lower = results[1]
    blended = ((upper + lower) * 0.5).astype(jnp.bfloat16)[None]
    local_gap = jnp.sum((upper - lower) * (upper + lower - 2.0 * goal)) / (
        row_count * lax.axis_size("ctx") * chan_count
    )
    factor = lax.psum(local_gap, "ctx") / (2.0 * NOISE_SCALE)
    local_term = factor * lax.dot_general(
        bottle, jitter, (((0,), (0,)), ((), ())), preferred_element_type=jnp.float32
    )
    grouped = lax.psum(local_term, "dp")
    estimate = lax.psum_scatter(grouped, "ctx", scatter_dimension=0, tiled=True)
    return (blended, estimate)


F32 = jnp.float32
BF16 = jnp.bfloat16
GROUP = 256
PHASES = ((0, 1), (1, 3), (4, 1))
HOPS = 4
EARLY = 2


def chip_at(position, chips):
    return jnp.where(position < chips // 2, 2 * position, 2 * (chips - 1 - position) + 1)


def kernel(
    chips,
    feats, bottle, noise, goal, entry, filters, leave,
    blended, estimate,
    weights, wpad, wpeer, fx, nx, bx, bo, gx, act, base, mixed, inner, mixed_late, inner_late,
    keep, csend, crecv, ysend, yrecv, zsend, zrecv, xsend, xrecv, pair, prow, gaps1, gaps2,
    ring_recv, x_recv, core_recv, bulk_send, init_send, init_recv, halo_send, halo_recv, rs_send, rs_recv, load,
):
    rows, chans = feats.shape
    bot = bottle.shape[1]
    share = entry.shape[0]
    unit = 2 * share
    half = chans // 2
    groups = chans // GROUP
    side = groups // 2
    zs = chips // 2
    others = chips - 1
    dp = lax.axis_index("dp")
    ctx = lax.axis_index("ctx")
    count = 2 * chips
    core = lax.rem(ctx, 2)
    chip = ctx // 2
    yy = lax.rem(chip, 2)
    zz = chip // 2
    par = lax.rem(dp, 2)
    mate = dp + 1 - 2 * par
    place = jnp.where(yy == 0, zz, chips - 1 - zz)

    def at(d, z, y, c):
        return {"dp": d, "ctx": (z * 2 + y) * 2 + c}

    def on_ring(p):
        return lax.rem(p + chips, chips)

    twin = at(dp, zz, yy, 1 - core)
    across = at(mate, zz, yy, core)
    near = [(i, j, k) for i in range(2) for j in range(2) for k in range(2) if i or j or k]

    def near_dev(i, j, k):
        return at(
            mate if i else dp,
            zz,
            1 - yy if j else yy,
            1 - core if k else core,
        )

    left = {"dp": dp, "ctx": lax.rem(ctx + count - 1, count)}
    right = {"dp": dp, "ctx": lax.rem(ctx + 1, count)}
    line = [at(dp, lax.rem(zz + d, zs), yy, core) for d in range(1, zs)]
    peers = [near_dev(*n) for n in near] + line + [left, right]

    w = DILATION
    middle = pl.ds(w, rows)
    loads = [
        pltpu.make_async_copy(src, dst, load.at[n])
        for n, (src, dst) in enumerate(
            (
                (bottle, bx.at[middle]), (noise, nx.at[middle]), (feats, fx.at[middle]), (goal, gx),
            )
        )
    ]
    for c in loads:
        c.start()
    blank = jnp.zeros((share, GROUP), F32)
    for g in range(groups):
        for m in range(5):
            shard = entry if m == 0 else leave if m == 4 else filters.at[m - 1]
            part = shard[:, g * GROUP:(g + 1) * GROUP].astype(F32)
            low = jnp.concatenate([part, blank], axis=0)
            high = jnp.concatenate([blank, part], axis=0)
            wpad[g, m] = jnp.where(core == 0, low, high).astype(BF16)

    barrier = pltpu.get_barrier_semaphore()
    for peer in peers:
        pl.semaphore_signal(barrier, inc=1, device_id=peer, device_id_type=pl.DeviceIdType.MESH)
    pl.semaphore_wait(barrier, len(peers))

    def remote(src, dst, ssem, rsem, dev):
        c = pltpu.make_async_remote_copy(
            src_ref=src, dst_ref=dst, send_sem=ssem, recv_sem=rsem,
            device_id=dev, device_id_type=pl.DeviceIdType.MESH,
        )
        return c

    def drain(ref, sem):
        pltpu.make_async_copy(ref, ref, sem).wait()

    mine = pl.ds(core * side, side)
    theirs = pl.ds((1 - core) * side, side)
    inits = []
    for n, (first, size) in enumerate(PHASES):
        inits.append(
            remote(
                wpad.at[theirs, pl.ds(first, size)], wpeer.at[theirs, pl.ds(first, size)],
                init_send.at[n], init_recv.at[n], twin,
            )
        )
    inits.append(remote(wpad.at[mine], wpeer.at[mine], init_send.at[3], init_recv.at[3], twin))
    for c in inits:
        c.start()
    to_left = []
    to_right = []
    for n, (src, dst) in enumerate(((feats, fx), (noise, nx), (bottle, bx))):
        to_left.append(
            remote(src.at[pl.ds(0, w)], dst.at[pl.ds(w + rows, w)], halo_send.at[2 * n], halo_recv.at[2 * n], left)
        )
        to_right.append(
            remote(src.at[pl.ds(rows - w, w)], dst.at[pl.ds(0, w)], halo_send.at[2 * n + 1], halo_recv.at[2 * n + 1], right)
        )

    @pl.when(ctx > 0)
    def _():
        for c in to_left:
            c.start()

    @pl.when(ctx < count - 1)
    def _():
        for c in to_right:
            c.start()

    @pl.when(ctx == 0)
    def _():
        for dst in (fx, nx, bx):
            dst[0:w, :] = jnp.zeros((w, dst.shape[1]), BF16)

    @pl.when(ctx == count - 1)
    def _():
        for dst in (fx, nx, bx):
            dst[w + rows:, :] = jnp.zeros((w, dst.shape[1]), BF16)

    def span(d, h):
        return pl.ds(unit * (0 if h == 0 else min(2 * h - 1 + d, chips - 1)), unit)

    def chip_of(k):
        return chip_at(on_ring(place if k == 0 else place - (k + 1) // 2 if k % 2 else place + k // 2), chips)

    g_pair = core * side + par
    g_mid = core * side + 1
    g_own = core * side + 2 * par
    g_x = core * side + 2 - 2 * par

    def piece(n, g, many, d, h):
        first, size = PHASES[n]
        return weights.at[pl.ds(g, many), pl.ds(first, size), span(d, h), :]

    def ring_piece(n, d, h, start):
        if h < HOPS:
            return piece(n, g_pair, 2, d, start)
        return piece(n, g_mid if d == 0 else g_own, 1, d, start)

    def toward(d):
        q = chip_at(on_ring(place + 1 if d == 0 else place - 1), chips)
        return {"dp": dp, "ctx": q * 2 + core}

    nexts = (toward(0), toward(1))

    def ring_copy(n, d, h):
        return remote(ring_piece(n, d, h, h - 1), ring_piece(n, d, h, h), bulk_send.at[0], ring_recv.at[n * 2 * HOPS + 2 * (h - 1) + d], nexts[d])

    def to_twin(n, h, p):
        late = 1 if n == 1 and h > EARLY else 0
        remote(p, p, bulk_send.at[2], core_recv.at[n + 2 * late], twin).start()

    def x_copy(n, d, h, g):
        p = piece(n, g, 1, d, h)
        return remote(p, p, bulk_send.at[1], x_recv.at[n * 2 * HOPS + 2 * (h - 1) + d], across)

    def hop(n, h):
        for d in range(2):
            ring_copy(n, d, h).wait_recv()
            if h < HOPS:
                ring_copy(n, d, h + 1).start()
            if h < HOPS or d == 1:
                x_copy(n, d, h, g_own).start()
        for d in range(2):
            to_twin(n, h, ring_piece(n, d, h, h))

    def xhop(n, h):
        for d in range(2):
            if h < HOPS or d == 1:
                x_copy(n, d, h, g_x).wait_recv()
                to_twin(n, h, piece(n, g_x, 1, d, h))

    def settle(n, sem, blocks):
        first, size = PHASES[n]
        drain(weights.at[pl.ds(0, side), pl.ds(first, size), pl.ds(0, blocks * unit)], core_recv.at[sem])

    def assemble(n, begin):
        first, size = PHASES[n]
        for g in range(side):
            for m in range(first, first + size):
                weights[begin + g, m, 0:unit, :] = wpad[begin + g, m] + wpeer[begin + g, m]

    def launch(n):
        p = remote(wpad.at[mine, pl.ds(*PHASES[n])], wpeer.at[mine, pl.ds(*PHASES[n])], init_send.at[n], init_recv.at[n], twin)
        p.wait_recv()
        assemble(n, core * side)
        for d in range(2):
            ring_copy(n, d, 1).start()

    launch(0)
    launch(1)
    for c in loads:
        c.wait()

    def outer(g):
        cols = pl.ds(pl.multiple_of(g * GROUP, GROUP), GROUP)
        return lax.dot_general(
            bx[middle, :], nx[middle, cols], (((0,), (0,)), ((), ())), preferred_element_type=F32
        ).reshape(chips, unit, GROUP)

    for g in range(side):
        csend[:, :, g * GROUP:(g + 1) * GROUP] = outer((1 - core) * side + g).astype(BF16)
    rs_core = remote(csend, crecv, rs_send.at[0], rs_recv.at[0], twin)
    rs_core.start()
    hop(0, 1)
    launch(2)
    for g in range(side):
        keep[:, :, g * GROUP:(g + 1) * GROUP] = outer(core * side + g)
    hop(0, 2)
    xhop(0, 1)
    hop(1, 1)
    rs_core.wait_recv()
    for z in range(zs):
        ysend[z] = (keep[2 * z + 1 - yy] + crecv[2 * z + 1 - yy].astype(F32)).astype(BF16)
    rs_y = remote(ysend, yrecv, rs_send.at[1], rs_recv.at[1], near_dev(0, 1, 0))
    rs_y.start()
    hop(0, 3)
    xhop(0, 2)
    remote(wpad.at[theirs], wpeer.at[theirs], init_send.at[3], init_recv.at[3], twin).wait_recv()
    for n in range(3):
        assemble(n, (1 - core) * side)
    hop(0, 4)
    xhop(0, 3)
    hop(1, 2)
    xhop(0, 4)
    xhop(1, 1)
    hop(2, 1)
    rs_y.wait_recv()
    for z in range(zs):
        total = keep[2 * z + yy] + crecv[2 * z + yy].astype(F32) + yrecv[z].astype(F32)
        keep[2 * z + yy] = total
        zsend[z] = total.astype(BF16)
    rs_z = []
    for d in range(1, zs):
        c = remote(zsend.at[lax.rem(zz + d, zs)], zrecv.at[d - 1], rs_send.at[1 + d], rs_recv.at[1 + d], line[d - 1])
        c.start()
        rs_z.append(c)

    @pl.when(ctx > 0)
    def _():
        for n in range(3):
            to_left[n].wait_send()
            to_right[n].wait_recv()

    @pl.when(ctx < count - 1)
    def _():
        for n in range(3):
            to_right[n].wait_send()
            to_left[n].wait_recv()

    order = lax.broadcasted_iota(jnp.int32, (bot, bot), 1)
    wanted = order
    for k in range(chips):
        wanted = jnp.where(order >= k * unit, order + (chip_of(k) - k) * unit, wanted)
    swap = jnp.where(lax.broadcasted_iota(jnp.int32, (bot, bot), 0) == wanted, 1.0, 0.0).astype(BF16)
    bo[...] = jnp.dot(bx[...], swap, preferred_element_type=F32).astype(BF16)
    settle(0, 0, others)

    edge = lax.broadcasted_iota(jnp.int32, (rows + 2 * w, 1), 0)
    inside = jnp.logical_and(
        jnp.logical_or(edge >= w, ctx > 0), jnp.logical_or(edge < w + rows, ctx < count - 1)
    )

    def enter(g):
        cols = pl.ds(g * GROUP, GROUP)
        b = fx[:, cols].astype(F32) + jnp.dot(bo[...], weights[g, 0], preferred_element_type=F32)
        off = nx[:, cols].astype(F32) * NOISE_SCALE
        base[:, cols] = b[w:w + rows]
        for p, state in enumerate((b + off, b - off)):
            act[p, :, cols] = jnp.where(inside, jax.nn.gelu(state), 0.0).astype(BF16)

    enter(0)
    hop(1, 3)
    xhop(1, 2)
    enter(1)
    hop(2, 2)
    xhop(2, 1)
    enter(2)
    enter(3)
    hop(1, 4)
    xhop(1, 3)
    enter(4)
    enter(5)
    hop(2, 3)
    xhop(1, 4)
    xhop(2, 2)
    soon = (2 * EARLY + 1) * unit
    settle(1, 1, 2 * EARLY)

    def mix(k, begin, size):
        total = jnp.zeros((2 * rows, size), F32)
        for g in range(groups):
            left_side = act[:, k * w:k * w + rows, g * GROUP:(g + 1) * GROUP].reshape(2 * rows, GROUP)
            total = total + lax.dot_general(
                left_side, weights[g, 1 + k, begin:begin + size, :],
                (((1,), (1,)), ((), ())), preferred_element_type=F32,
            )
        return total

    mixed[...] = mix(0, 0, soon)
    hop(2, 4)
    xhop(2, 3)
    mixed[...] += mix(1, 0, soon)
    for c in rs_z:
        c.wait_recv()
    owned = keep[chip]
    for d in range(zs - 1):
        owned = owned + zrecv[d].astype(F32)
    pair[par] = owned
    xsend[...] = owned.astype(BF16)
    rs_x = remote(xsend, xrecv, rs_send.at[1 + zs], rs_recv.at[1 + zs], across)
    rs_x.start()
    xhop(2, 4)
    inner[...] = jax.nn.gelu(mixed[...] + mix(2, 0, soon)).astype(BF16)
    settle(1, 3, others - 2 * EARLY)
    mixed_late[...] = mix(0, soon, bot - soon)
    mixed_late[...] += mix(1, soon, bot - soon)
    inner_late[...] = jax.nn.gelu(mixed_late[...] + mix(2, soon, bot - soon)).astype(BF16)
    rs_x.wait_recv()
    pair[1 - par] = xrecv[...].astype(F32)
    give = pl.ds(pl.multiple_of((1 - core) * (unit // 2), 8), unit // 2)
    have = pl.ds(pl.multiple_of(core * (unit // 2), 8), unit // 2)
    rs_f = remote(pair.at[:, give, :], prow, rs_send.at[2 + zs], rs_recv.at[2 + zs], twin)
    rs_f.start()
    settle(2, 2, others)

    lanes = jnp.zeros((1, GROUP), F32)
    for g in range(groups):
        cols = pl.ds(g * GROUP, GROUP)
        off = nx[middle, cols].astype(F32) * NOISE_SCALE
        b = base[:, cols]
        outs = jnp.dot(inner[...], weights[g, 4, 0:soon, :], preferred_element_type=F32)
        outs = outs + jnp.dot(inner_late[...], weights[g, 4, soon:bot, :], preferred_element_type=F32)
        upper = b + off + outs[:rows]
        lower = b - off + outs[rows:]
        both = upper + lower
        blended[:, cols] = (both * 0.5).astype(BF16)
        lanes = lanes + jnp.sum((upper - lower) * (both - 2.0 * gx[:, cols].astype(F32)), axis=0, keepdims=True)
    local = jnp.sum(lanes, axis=1, keepdims=True) / (rows * count * chans)
    shelf = lax.broadcasted_iota(jnp.int32, (8, 128), 0)
    gaps1[0] = jnp.where(shelf == par, local, 0.0)
    sent = []
    for i, n in enumerate(near):
        c = remote(gaps1.at[0], gaps1.at[i + 1], bulk_send.at[3], bulk_send.at[4], near_dev(*n))
        c.start()
    drain(gaps1.at[pl.ds(1, len(near))], bulk_send.at[4])
    drain(gaps1.at[pl.ds(1, len(near))], bulk_send.at[3])
    gaps2[0] = jnp.sum(gaps1[...], axis=0)
    for d in range(1, zs):
        remote(gaps2.at[0], gaps2.at[d], bulk_send.at[5], bulk_send.at[6], line[d - 1]).start()
    rs_f.wait()
    drain(gaps2.at[pl.ds(1, zs - 1)], bulk_send.at[6])
    drain(gaps2.at[pl.ds(1, zs - 1)], bulk_send.at[5])
    factors = jnp.sum(gaps2[...], axis=0) / (2.0 * NOISE_SCALE)
    f0 = factors[0:1, 0:1]
    f1 = factors[1:2, 0:1]
    here = pl.ds(pl.multiple_of(core * half, 128), half)
    there = pl.ds(pl.multiple_of((1 - core) * half, 128), half)
    estimate[:, here] = f0 * pair[0, have, :] + f1 * pair[1, have, :]
    estimate[:, there] = f0 * prow[0] + f1 * prow[1]

    rs_core.wait_send()
    rs_y.wait_send()
    rs_x.wait_send()
    for c in rs_z:
        c.wait_send()
    for c in inits:
        c.wait_send()
    for n, ways in enumerate((2, 1, 3)):
        drain(weights.at[pl.ds(0, ways), :, pl.ds(0, others * unit)], bulk_send.at[n])


def fused(features, bottleneck, node_noise, targets, entry_weight, conv_filters, exit_weight):
    count = lax.axis_size("ctx")
    chips = count // 2
    _, rows, chans = features.shape
    bot = bottleneck.shape[2]
    share = entry_weight.shape[0]
    unit = 2 * share
    groups = chans // GROUP
    zs = chips // 2
    wide = rows + 2 * DILATION
    half = chans // 2
    soon = (2 * EARLY + 1) * unit
    blended, estimate = pl.pallas_call(
        functools.partial(kernel, chips),
        out_shape=(
            jax.ShapeDtypeStruct((rows, chans), BF16),
            jax.ShapeDtypeStruct((share, chans), F32),
        ),
        in_specs=[pl.BlockSpec(memory_space=pltpu.HBM)] * 4 + [pl.BlockSpec(memory_space=pltpu.VMEM)] * 3,
        out_specs=[pl.BlockSpec(memory_space=pltpu.VMEM)] * 2,
        scratch_shapes=[
            pltpu.VMEM((groups, 5, bot, GROUP), BF16),
            pltpu.VMEM((groups, 5, unit, GROUP), BF16),
            pltpu.VMEM((groups, 5, unit, GROUP), BF16),
            pltpu.VMEM((wide, chans), BF16),
            pltpu.VMEM((wide, chans), BF16),
            pltpu.VMEM((wide, bot), BF16),
            pltpu.VMEM((wide, bot), BF16),
            pltpu.VMEM((rows, chans), BF16),
            pltpu.VMEM((2, wide, chans), BF16),
            pltpu.VMEM((rows, chans), F32),
            pltpu.VMEM((2 * rows, soon), F32),
            pltpu.VMEM((2 * rows, soon), BF16),
            pltpu.VMEM((2 * rows, bot - soon), F32),
            pltpu.VMEM((2 * rows, bot - soon), BF16),
            pltpu.VMEM((chips, unit, half), F32),
            pltpu.VMEM((chips, unit, half), BF16),
            pltpu.VMEM((chips, unit, half), BF16),
            pltpu.VMEM((zs, unit, half), BF16),
            pltpu.VMEM((zs, unit, half), BF16),
            pltpu.VMEM((zs, unit, half), BF16),
            pltpu.VMEM((zs - 1, unit, half), BF16),
            pltpu.VMEM((unit, half), BF16),
            pltpu.VMEM((unit, half), BF16),
            pltpu.VMEM((2, unit, half), F32),
            pltpu.VMEM((2, unit // 2, half), F32),
            pltpu.VMEM((8, 8, 128), F32),
            pltpu.VMEM((zs, 8, 128), F32),
            pltpu.SemaphoreType.DMA((3 * 2 * HOPS,)),
            pltpu.SemaphoreType.DMA((3 * 2 * HOPS,)),
            pltpu.SemaphoreType.DMA((4,)),
            pltpu.SemaphoreType.DMA((7,)),
            pltpu.SemaphoreType.DMA((4,)),
            pltpu.SemaphoreType.DMA((4,)),
            pltpu.SemaphoreType.DMA((6,)),
            pltpu.SemaphoreType.DMA((6,)),
            pltpu.SemaphoreType.DMA((3 + zs,)),
            pltpu.SemaphoreType.DMA((3 + zs,)),
            pltpu.SemaphoreType.DMA((4,)),
        ],
        compiler_params=pltpu.CompilerParams(
            collective_id=0, has_side_effects=True, vmem_limit_bytes=59 * 1024 * 1024
        ),
    )(
        features[0], bottleneck[0], node_noise[0], targets[0],
        entry_weight, jnp.swapaxes(conv_filters, 1, 2), exit_weight,
    )
    return blended[None], estimate


def solution(mesh):
    small = mesh.shape["ctx"] == 16 and mesh.shape["dp"] == 2
    return jax.shard_map(
        fused if small else body,
        mesh=mesh,
        in_specs=(
            P("dp", "ctx", None),
            P("dp", "ctx", None),
            P("dp", "ctx", None),
            P("dp", "ctx", None),
            P("ctx", None),
            P(None, None, "ctx"),
            P("ctx", None),
        ),
        out_specs=(P("dp", "ctx", None), P("ctx", None)),
        check_vma=False,
    )
```

```python
import functools

import jax
import jax.numpy as jnp
from jax import lax
from jax.experimental import pallas as pl
from jax.experimental.pallas import tpu as pltpu
from jax.sharding import PartitionSpec as P

DILATION = 32


NOISE_SCALE = 0.1


def padded_2(cells, sides, width):
    for axis, dim in sides:
        count = lax.axis_size(axis)
        ends = count - 1
        head = lax.slice_in_dim(cells, 0, width, axis=dim)
        tail = lax.slice_in_dim(cells, cells.shape[dim] - width, cells.shape[dim], axis=dim)
        cells = jnp.concatenate(
            [
                lax.ppermute(tail, axis, [(i, (i + 1) % count) for i in range(ends)]),
                cells,
                lax.ppermute(head, axis, [((i + 1) % count, i) for i in range(ends)]),
            ],
            axis=dim,
        )
    return cells


def taps_for(padded, row_count, spacing, portion):
    summed = jnp.dot(padded[..., 0:row_count, :], portion[0], preferred_element_type=jnp.float32)
    summed = summed + jnp.dot(
        padded[..., spacing : spacing + row_count, :],
        portion[1],
        preferred_element_type=jnp.float32,
    )
    summed = summed + jnp.dot(
        padded[..., 2 * spacing : 2 * spacing + row_count, :],
        portion[2],
        preferred_element_type=jnp.float32,
    )
    return summed


def rows_for(left_side, portion):
    return jnp.dot(left_side, portion, preferred_element_type=jnp.float32)


def body(features, bottleneck, node_noise, targets, entry_weight, conv_filters, exit_weight):
    feats = features[0]
    bottle = bottleneck[0]
    jitter = node_noise[0]
    goal = targets[0].astype(jnp.float32)
    row_count = feats.shape[0]
    chan_count = feats.shape[1]
    spacing = DILATION
    baseline = feats.astype(jnp.float32) + rows_for(
        bottle, lax.all_gather(entry_weight, "ctx", axis=0, tiled=True)
    )
    offset_field = jitter.astype(jnp.float32) * NOISE_SCALE
    results = []
    for polarity in (1.0, -1.0):
        state = baseline + polarity * offset_field
        activated = jax.nn.gelu(state).astype(jnp.bfloat16)
        padded = padded_2(activated, (("ctx", 0),), spacing)
        mixed = taps_for(
            padded, row_count, spacing, lax.all_gather(conv_filters, "ctx", axis=2, tiled=True)
        )
        inner = jax.nn.gelu(mixed).astype(jnp.bfloat16)
        results.append(
            state + rows_for(inner, lax.all_gather(exit_weight, "ctx", axis=0, tiled=True))
        )
    upper = results[0]
    lower = results[1]
    blended = ((upper + lower) * 0.5).astype(jnp.bfloat16)[None]
    local_gap = jnp.sum((upper - lower) * (upper + lower - 2.0 * goal)) / (
        row_count * lax.axis_size("ctx") * chan_count
    )
    factor = lax.psum(local_gap, "ctx") / (2.0 * NOISE_SCALE)
    local_term = factor * lax.dot_general(
        bottle, jitter, (((0,), (0,)), ((), ())), preferred_element_type=jnp.float32
    )
    grouped = lax.psum(local_term, "dp")
    estimate = lax.psum_scatter(grouped, "ctx", scatter_dimension=0, tiled=True)
    return (blended, estimate)


F32 = jnp.float32
BF16 = jnp.bfloat16
GROUP = 256
PHASES = ((0, 1), (1, 3), (4, 1))


def kernel(
    chips,
    feats, bottle, noise, goal, entry, filters, leave,
    blended, estimate,
    weights, wpad, wpeer, fx, nx, bx, bo, gx, act, base, mixed, inner, mixed_late, inner_late,
    keep, csend, crecv, ysend, yrecv, zsend, zrecv, xsend, xrecv, pair, prow, gaps1, gaps2,
    ring_recv, x_recv, core_recv, bulk_send, init_send, init_recv, halo_send, halo_recv, rs_send, rs_recv, load,
):
    rows, chans = feats.shape
    bot = bottle.shape[1]
    share = entry.shape[0]
    unit = 2 * share
    half = chans // 2
    groups = chans // GROUP
    side = groups // 2
    zs = chips // 2
    others = chips - 1
    dp = lax.axis_index("dp")
    ctx = lax.axis_index("ctx")
    count = 2 * chips
    core = lax.rem(ctx, 2)
    chip = ctx // 2
    yy = lax.rem(chip, 2)
    zz = chip // 2
    par = lax.rem(dp, 2)
    mate = dp + 1 - 2 * par

    def at(d, z, y, c):
        return {"dp": d, "ctx": (z * 2 + y) * 2 + c}

    twin = at(dp, zz, yy, 1 - core)
    across = at(mate, zz, yy, core)
    near = [(i, j, k) for i in range(2) for j in range(2) for k in range(2) if i or j or k]

    def near_dev(i, j, k):
        return at(
            mate if i else dp,
            zz,
            1 - yy if j else yy,
            1 - core if k else core,
        )

    left = {"dp": dp, "ctx": lax.rem(ctx + count - 1, count)}
    right = {"dp": dp, "ctx": lax.rem(ctx + 1, count)}
    line = [at(dp, lax.rem(zz + d, zs), yy, core) for d in range(1, zs)]
    peers = [near_dev(*n) for n in near] + line + [left, right]

    w = DILATION
    middle = pl.ds(w, rows)
    loads = [
        pltpu.make_async_copy(src, dst, load.at[n])
        for n, (src, dst) in enumerate(
            (
                (bottle, bx.at[middle]), (noise, nx.at[middle]), (feats, fx.at[middle]), (goal, gx),
            )
        )
    ]
    for c in loads:
        c.start()
    barrier = pltpu.get_barrier_semaphore()
    for peer in peers:
        pl.semaphore_signal(barrier, inc=1, device_id=peer, device_id_type=pl.DeviceIdType.MESH)
    blank = jnp.zeros((share, GROUP), F32)
    for g in range(groups):
        for m in range(5):
            shard = entry if m == 0 else leave if m == 4 else filters.at[m - 1]
            part = shard[:, g * GROUP:(g + 1) * GROUP].astype(F32)
            low = jnp.concatenate([part, blank], axis=0)
            high = jnp.concatenate([blank, part], axis=0)
            wpad[g, m] = jnp.where(core == 0, low, high).astype(BF16)
    pl.semaphore_wait(barrier, len(peers))

    def remote(src, dst, ssem, rsem, dev):
        c = pltpu.make_async_remote_copy(
            src_ref=src, dst_ref=dst, send_sem=ssem, recv_sem=rsem,
            device_id=dev, device_id_type=pl.DeviceIdType.MESH,
        )
        return c

    def drain(ref, sem):
        pltpu.make_async_copy(ref, ref, sem).wait()

    mine = pl.ds(core * side, side)
    theirs = pl.ds((1 - core) * side, side)
    inits = []
    for n, (first, size) in enumerate(PHASES):
        inits.append(
            remote(
                wpad.at[theirs, pl.ds(first, size)], wpeer.at[theirs, pl.ds(first, size)],
                init_send.at[n], init_recv.at[n], twin,
            )
        )
    inits.append(remote(wpad.at[mine], wpeer.at[mine], init_send.at[3], init_recv.at[3], twin))
    for c in inits:
        c.start()
    to_left = []
    to_right = []
    for n, (src, dst) in enumerate(((feats, fx), (noise, nx), (bottle, bx))):
        to_left.append(
            remote(src.at[pl.ds(0, w)], dst.at[pl.ds(w + rows, w)], halo_send.at[2 * n], halo_recv.at[2 * n], left)
        )
        to_right.append(
            remote(src.at[pl.ds(rows - w, w)], dst.at[pl.ds(0, w)], halo_send.at[2 * n + 1], halo_recv.at[2 * n + 1], right)
        )

    @pl.when(ctx > 0)
    def _():
        for c in to_left:
            c.start()

    @pl.when(ctx < count - 1)
    def _():
        for c in to_right:
            c.start()

    @pl.when(ctx == 0)
    def _():
        for dst in (fx, nx, bx):
            dst[0:w, :] = jnp.zeros((w, dst.shape[1]), BF16)

    @pl.when(ctx == count - 1)
    def _():
        for dst in (fx, nx, bx):
            dst[w + rows:, :] = jnp.zeros((w, dst.shape[1]), BF16)

    def chip_of(k):
        return lax.rem(zz + zs - k % zs, zs) * 2 + (yy if k < zs else 1 - yy)

    g_pair = core * side + par
    g_mid = core * side + 1
    g_own = core * side + 2 * par
    g_x = core * side + 2 - 2 * par

    def piece(n, g, many, k):
        first, size = PHASES[n]
        return weights.at[pl.ds(g, many), pl.ds(first, size), pl.ds(k * unit, unit), :]

    beside = near_dev(0, 1, 0)

    def plane_copy(n, k):
        dst = piece(n, g_pair, 2, k)
        src = piece(n, g_pair, 2, 0 if k < zs else k - zs)
        return remote(src, dst, bulk_send.at[0], ring_recv.at[n * others + k - 1], line[k - 1] if k < zs else beside)

    def to_twin(n, k, p):
        late = 1 if n == 1 and k > zs else 0
        remote(p, p, bulk_send.at[2], core_recv.at[n + 2 * late], twin).start()

    def x_copy(n, k, g):
        p = piece(n, g, 1, k)
        return remote(p, p, bulk_send.at[1], x_recv.at[n * others + k - 1], across)

    def hop(n, ks):
        for k in ks:
            plane_copy(n, k).wait_recv()
            if k < zs:
                plane_copy(n, k + zs).start()
            x_copy(n, k, g_own).start()
            to_twin(n, k, piece(n, g_pair, 2, k))

    def xhop(n, ks):
        for k in ks:
            x_copy(n, k, g_x).wait_recv()
            to_twin(n, k, piece(n, g_x, 1, k))

    first_half = range(1, zs + 1)
    last_half = range(zs + 1, chips)

    def settle(n, sem, blocks):
        first, size = PHASES[n]
        drain(weights.at[pl.ds(0, side), pl.ds(first, size), pl.ds(0, blocks * unit)], core_recv.at[sem])

    def assemble(n, begin):
        first, size = PHASES[n]
        for g in range(side):
            for m in range(first, first + size):
                weights[begin + g, m, 0:unit, :] = wpad[begin + g, m] + wpeer[begin + g, m]

    def launch(n):
        p = remote(wpad.at[mine, pl.ds(*PHASES[n])], wpeer.at[mine, pl.ds(*PHASES[n])], init_send.at[n], init_recv.at[n], twin)
        p.wait_recv()
        assemble(n, core * side)
        for k in range(1, zs + 1):
            plane_copy(n, k).start()

    launch(0)
    launch(1)
    for c in loads:
        c.wait()

    def outer(g):
        cols = pl.ds(pl.multiple_of(g * GROUP, GROUP), GROUP)
        return lax.dot_general(
            bx[middle, :], nx[middle, cols], (((0,), (0,)), ((), ())), preferred_element_type=F32
        ).reshape(chips, unit, GROUP)

    for g in range(side):
        csend[:, :, g * GROUP:(g + 1) * GROUP] = outer((1 - core) * side + g).astype(BF16)
    rs_core = remote(csend, crecv, rs_send.at[0], rs_recv.at[0], twin)
    rs_core.start()
    launch(2)
    hop(0, first_half)
    for g in range(side):
        keep[:, :, g * GROUP:(g + 1) * GROUP] = outer(core * side + g)
    hop(0, last_half)
    xhop(0, first_half)
    rs_core.wait_recv()
    for z in range(zs):
        ysend[z] = (keep[2 * z + 1 - yy] + crecv[2 * z + 1 - yy].astype(F32)).astype(BF16)
    rs_y = remote(ysend, yrecv, rs_send.at[1], rs_recv.at[1], near_dev(0, 1, 0))
    rs_y.start()
    remote(wpad.at[theirs], wpeer.at[theirs], init_send.at[3], init_recv.at[3], twin).wait_recv()
    for n in range(3):
        assemble(n, (1 - core) * side)
    xhop(0, last_half)

    @pl.when(ctx > 0)
    def _():
        for n in range(3):
            to_left[n].wait_send()
            to_right[n].wait_recv()

    @pl.when(ctx < count - 1)
    def _():
        for n in range(3):
            to_right[n].wait_send()
            to_left[n].wait_recv()

    order = lax.broadcasted_iota(jnp.int32, (bot, bot), 1)
    wanted = order
    for k in range(chips):
        wanted = jnp.where(order >= k * unit, order + (chip_of(k) - k) * unit, wanted)
    swap = jnp.where(lax.broadcasted_iota(jnp.int32, (bot, bot), 0) == wanted, 1.0, 0.0).astype(BF16)
    bo[...] = jnp.dot(bx[...], swap, preferred_element_type=F32).astype(BF16)
    settle(0, 0, others)

    edge = lax.broadcasted_iota(jnp.int32, (rows + 2 * w, 1), 0)
    inside = jnp.logical_and(
        jnp.logical_or(edge >= w, ctx > 0), jnp.logical_or(edge < w + rows, ctx < count - 1)
    )

    def enter(g):
        cols = pl.ds(g * GROUP, GROUP)
        b = fx[:, cols].astype(F32) + jnp.dot(bo[...], weights[g, 0], preferred_element_type=F32)
        off = nx[:, cols].astype(F32) * NOISE_SCALE
        base[:, cols] = b[w:w + rows]
        for p, state in enumerate((b + off, b - off)):
            act[p, :, cols] = jnp.where(inside, jax.nn.gelu(state), 0.0).astype(BF16)

    enter(0)
    hop(1, range(1, 2))
    enter(1)
    hop(1, range(2, 3))
    enter(2)
    hop(1, range(3, zs + 1))
    enter(3)
    rs_y.wait_recv()
    for z in range(zs):
        total = keep[2 * z + yy] + crecv[2 * z + yy].astype(F32) + yrecv[z].astype(F32)
        keep[2 * z + yy] = total
        zsend[z] = total.astype(BF16)
    rs_z = []
    for d in range(1, zs):
        c = remote(zsend.at[lax.rem(zz + d, zs)], zrecv.at[d - 1], rs_send.at[1 + d], rs_recv.at[1 + d], line[d - 1])
        c.start()
        rs_z.append(c)
    hop(2, first_half)
    xhop(1, first_half)
    enter(4)
    enter(5)
    hop(1, last_half)
    soon = (zs + 1) * unit
    settle(1, 1, zs)

    def mix(k, begin, size):
        total = jnp.zeros((2 * rows, size), F32)
        for g in range(groups):
            left_side = act[:, k * w:k * w + rows, g * GROUP:(g + 1) * GROUP].reshape(2 * rows, GROUP)
            total = total + lax.dot_general(
                left_side, weights[g, 1 + k, begin:begin + size, :],
                (((1,), (1,)), ((), ())), preferred_element_type=F32,
            )
        return total

    mixed[...] = mix(0, 0, soon)
    hop(2, last_half)
    xhop(1, last_half)
    xhop(2, first_half)
    mixed[...] += mix(1, 0, soon)
    for c in rs_z:
        c.wait_recv()
    owned = keep[chip]
    for d in range(zs - 1):
        owned = owned + zrecv[d].astype(F32)
    pair[par] = owned
    xsend[...] = owned.astype(BF16)
    rs_x = remote(xsend, xrecv, rs_send.at[1 + zs], rs_recv.at[1 + zs], across)
    rs_x.start()
    xhop(2, last_half)
    inner[...] = jax.nn.gelu(mixed[...] + mix(2, 0, soon)).astype(BF16)
    settle(1, 3, others - zs)
    mixed_late[...] = mix(0, soon, bot - soon)
    mixed_late[...] += mix(1, soon, bot - soon)
    inner_late[...] = jax.nn.gelu(mixed_late[...] + mix(2, soon, bot - soon)).astype(BF16)
    rs_x.wait_recv()
    pair[1 - par] = xrecv[...].astype(F32)
    give = pl.ds(pl.multiple_of((1 - core) * (unit // 2), 8), unit // 2)
    have = pl.ds(pl.multiple_of(core * (unit // 2), 8), unit // 2)
    rs_f = remote(pair.at[:, give, :], prow, rs_send.at[2 + zs], rs_recv.at[2 + zs], twin)
    rs_f.start()
    settle(2, 2, others)

    lanes = jnp.zeros((1, GROUP), F32)
    for g in range(groups):
        cols = pl.ds(g * GROUP, GROUP)
        off = nx[middle, cols].astype(F32) * NOISE_SCALE
        b = base[:, cols]
        outs = jnp.dot(inner[...], weights[g, 4, 0:soon, :], preferred_element_type=F32)
        outs = outs + jnp.dot(inner_late[...], weights[g, 4, soon:bot, :], preferred_element_type=F32)
        upper = b + off + outs[:rows]
        lower = b - off + outs[rows:]
        both = upper + lower
        blended[:, cols] = (both * 0.5).astype(BF16)
        lanes = lanes + jnp.sum((upper - lower) * (both - 2.0 * gx[:, cols].astype(F32)), axis=0, keepdims=True)
    local = jnp.sum(lanes, axis=1, keepdims=True) / (rows * count * chans)
    shelf = lax.broadcasted_iota(jnp.int32, (8, 128), 0)
    gaps1[0] = jnp.where(shelf == par, local, 0.0)
    sent = []
    for i, n in enumerate(near):
        c = remote(gaps1.at[0], gaps1.at[i + 1], bulk_send.at[3], bulk_send.at[4], near_dev(*n))
        c.start()
    drain(gaps1.at[pl.ds(1, len(near))], bulk_send.at[4])
    drain(gaps1.at[pl.ds(1, len(near))], bulk_send.at[3])
    gaps2[0] = jnp.sum(gaps1[...], axis=0)
    for d in range(1, zs):
        remote(gaps2.at[0], gaps2.at[d], bulk_send.at[5], bulk_send.at[6], line[d - 1]).start()
    rs_f.wait()
    drain(gaps2.at[pl.ds(1, zs - 1)], bulk_send.at[6])
    drain(gaps2.at[pl.ds(1, zs - 1)], bulk_send.at[5])
    factors = jnp.sum(gaps2[...], axis=0) / (2.0 * NOISE_SCALE)
    f0 = factors[0:1, 0:1]
    f1 = factors[1:2, 0:1]
    here = pl.ds(pl.multiple_of(core * half, 128), half)
    there = pl.ds(pl.multiple_of((1 - core) * half, 128), half)
    estimate[:, here] = f0 * pair[0, have, :] + f1 * pair[1, have, :]
    estimate[:, there] = f0 * prow[0] + f1 * prow[1]

    rs_core.wait_send()
    rs_y.wait_send()
    rs_x.wait_send()
    for c in rs_z:
        c.wait_send()
    for c in inits:
        c.wait_send()
    for n, ways in enumerate((2, 1, 3)):
        drain(weights.at[pl.ds(0, ways), :, pl.ds(0, others * unit)], bulk_send.at[n])


def fused(features, bottleneck, node_noise, targets, entry_weight, conv_filters, exit_weight):
    count = lax.axis_size("ctx")
    chips = count // 2
    _, rows, chans = features.shape
    bot = bottleneck.shape[2]
    share = entry_weight.shape[0]
    unit = 2 * share
    groups = chans // GROUP
    zs = chips // 2
    wide = rows + 2 * DILATION
    half = chans // 2
    soon = (zs + 1) * unit
    blended, estimate = pl.pallas_call(
        functools.partial(kernel, chips),
        out_shape=(
            jax.ShapeDtypeStruct((rows, chans), BF16),
            jax.ShapeDtypeStruct((share, chans), F32),
        ),
        in_specs=[pl.BlockSpec(memory_space=pltpu.HBM)] * 4 + [pl.BlockSpec(memory_space=pltpu.VMEM)] * 3,
        out_specs=[pl.BlockSpec(memory_space=pltpu.VMEM)] * 2,
        scratch_shapes=[
            pltpu.VMEM((groups, 5, bot, GROUP), BF16),
            pltpu.VMEM((groups, 5, unit, GROUP), BF16),
            pltpu.VMEM((groups, 5, unit, GROUP), BF16),
            pltpu.VMEM((wide, chans), BF16),
            pltpu.VMEM((wide, chans), BF16),
            pltpu.VMEM((wide, bot), BF16),
            pltpu.VMEM((wide, bot), BF16),
            pltpu.VMEM((rows, chans), BF16),
            pltpu.VMEM((2, wide, chans), BF16),
            pltpu.VMEM((rows, chans), F32),
            pltpu.VMEM((2 * rows, soon), F32),
            pltpu.VMEM((2 * rows, soon), BF16),
            pltpu.VMEM((2 * rows, bot - soon), F32),
            pltpu.VMEM((2 * rows, bot - soon), BF16),
            pltpu.VMEM((chips, unit, half), F32),
            pltpu.VMEM((chips, unit, half), BF16),
            pltpu.VMEM((chips, unit, half), BF16),
            pltpu.VMEM((zs, unit, half), BF16),
            pltpu.VMEM((zs, unit, half), BF16),
            pltpu.VMEM((zs, unit, half), BF16),
            pltpu.VMEM((zs - 1, unit, half), BF16),
            pltpu.VMEM((unit, half), BF16),
            pltpu.VMEM((unit, half), BF16),
            pltpu.VMEM((2, unit, half), F32),
            pltpu.VMEM((2, unit // 2, half), F32),
            pltpu.VMEM((8, 8, 128), F32),
            pltpu.VMEM((zs, 8, 128), F32),
            pltpu.SemaphoreType.DMA((3 * (chips - 1),)),
            pltpu.SemaphoreType.DMA((3 * (chips - 1),)),
            pltpu.SemaphoreType.DMA((4,)),
            pltpu.SemaphoreType.DMA((7,)),
            pltpu.SemaphoreType.DMA((4,)),
            pltpu.SemaphoreType.DMA((4,)),
            pltpu.SemaphoreType.DMA((6,)),
            pltpu.SemaphoreType.DMA((6,)),
            pltpu.SemaphoreType.DMA((3 + zs,)),
            pltpu.SemaphoreType.DMA((3 + zs,)),
            pltpu.SemaphoreType.DMA((4,)),
        ],
        compiler_params=pltpu.CompilerParams(
            collective_id=0, has_side_effects=True, vmem_limit_bytes=59 * 1024 * 1024
        ),
    )(
        features[0], bottleneck[0], node_noise[0], targets[0],
        entry_weight, jnp.swapaxes(conv_filters, 1, 2), exit_weight,
    )
    return blended[None], estimate


def solution(mesh):
    small = mesh.shape["ctx"] == 16 and mesh.shape["dp"] == 2
    return jax.shard_map(
        fused if small else body,
        mesh=mesh,
        in_specs=(
            P("dp", "ctx", None),
            P("dp", "ctx", None),
            P("dp", "ctx", None),
            P("dp", "ctx", None),
            P("ctx", None),
            P(None, None, "ctx"),
            P("ctx", None),
        ),
        out_specs=(P("dp", "ctx", None), P("ctx", None)),
        check_vma=False,
    )
```

```python
import functools

import jax
import jax.numpy as jnp
from jax import lax
from jax.experimental import pallas as pl
from jax.experimental.pallas import tpu as pltpu
from jax.sharding import PartitionSpec as P

DILATION = 32


NOISE_SCALE = 0.1


def padded_2(cells, sides, width):
    for axis, dim in sides:
        count = lax.axis_size(axis)
        ends = count - 1
        head = lax.slice_in_dim(cells, 0, width, axis=dim)
        tail = lax.slice_in_dim(cells, cells.shape[dim] - width, cells.shape[dim], axis=dim)
        cells = jnp.concatenate(
            [
                lax.ppermute(tail, axis, [(i, (i + 1) % count) for i in range(ends)]),
                cells,
                lax.ppermute(head, axis, [((i + 1) % count, i) for i in range(ends)]),
            ],
            axis=dim,
        )
    return cells


def taps_for(padded, row_count, spacing, portion):
    summed = jnp.dot(padded[..., 0:row_count, :], portion[0], preferred_element_type=jnp.float32)
    summed = summed + jnp.dot(
        padded[..., spacing : spacing + row_count, :],
        portion[1],
        preferred_element_type=jnp.float32,
    )
    summed = summed + jnp.dot(
        padded[..., 2 * spacing : 2 * spacing + row_count, :],
        portion[2],
        preferred_element_type=jnp.float32,
    )
    return summed


def rows_for(left_side, portion):
    return jnp.dot(left_side, portion, preferred_element_type=jnp.float32)


def body(features, bottleneck, node_noise, targets, entry_weight, conv_filters, exit_weight):
    feats = features[0]
    bottle = bottleneck[0]
    jitter = node_noise[0]
    goal = targets[0].astype(jnp.float32)
    row_count = feats.shape[0]
    chan_count = feats.shape[1]
    spacing = DILATION
    baseline = feats.astype(jnp.float32) + rows_for(
        bottle, lax.all_gather(entry_weight, "ctx", axis=0, tiled=True)
    )
    offset_field = jitter.astype(jnp.float32) * NOISE_SCALE
    results = []
    for polarity in (1.0, -1.0):
        state = baseline + polarity * offset_field
        activated = jax.nn.gelu(state).astype(jnp.bfloat16)
        padded = padded_2(activated, (("ctx", 0),), spacing)
        mixed = taps_for(
            padded, row_count, spacing, lax.all_gather(conv_filters, "ctx", axis=2, tiled=True)
        )
        inner = jax.nn.gelu(mixed).astype(jnp.bfloat16)
        results.append(
            state + rows_for(inner, lax.all_gather(exit_weight, "ctx", axis=0, tiled=True))
        )
    upper = results[0]
    lower = results[1]
    blended = ((upper + lower) * 0.5).astype(jnp.bfloat16)[None]
    local_gap = jnp.sum((upper - lower) * (upper + lower - 2.0 * goal)) / (
        row_count * lax.axis_size("ctx") * chan_count
    )
    factor = lax.psum(local_gap, "ctx") / (2.0 * NOISE_SCALE)
    local_term = factor * lax.dot_general(
        bottle, jitter, (((0,), (0,)), ((), ())), preferred_element_type=jnp.float32
    )
    grouped = lax.psum(local_term, "dp")
    estimate = lax.psum_scatter(grouped, "ctx", scatter_dimension=0, tiled=True)
    return (blended, estimate)


F32 = jnp.float32
BF16 = jnp.bfloat16
GROUP = 256
PHASES = ((0, 1), (1, 3), (4, 1))


def kernel(
    chips,
    feats, bottle, noise, goal, entry, filters, leave,
    blended, estimate,
    weights, wpad, wpeer, fx, nx, bx, bo, gx, act, base, mixed, inner, mixed_late, inner_late,
    keep, csend, crecv, ysend, yrecv, zsend, zrecv, xsend, xrecv, pair, prow, gaps1, gaps2,
    ring_recv, x_recv, core_recv, bulk_send, init_send, init_recv, halo_send, halo_recv, rs_send, rs_recv, load,
):
    rows, chans = feats.shape
    bot = bottle.shape[1]
    share = entry.shape[0]
    unit = 2 * share
    half = chans // 2
    groups = chans // GROUP
    side = groups // 2
    zs = chips // 2
    others = chips - 1
    dp = lax.axis_index("dp")
    ctx = lax.axis_index("ctx")
    count = 2 * chips
    core = lax.rem(ctx, 2)
    chip = ctx // 2
    yy = lax.rem(chip, 2)
    zz = chip // 2
    par = lax.rem(dp, 2)
    mate = dp + 1 - 2 * par

    def at(d, z, y, c):
        return {"dp": d, "ctx": (z * 2 + y) * 2 + c}

    twin = at(dp, zz, yy, 1 - core)
    across = at(mate, zz, yy, core)
    near = [(i, j, k) for i in range(2) for j in range(2) for k in range(2) if i or j or k]

    def near_dev(i, j, k):
        return at(
            mate if i else dp,
            zz,
            1 - yy if j else yy,
            1 - core if k else core,
        )

    left = {"dp": dp, "ctx": lax.rem(ctx + count - 1, count)}
    right = {"dp": dp, "ctx": lax.rem(ctx + 1, count)}
    line = [at(dp, lax.rem(zz + d, zs), yy, core) for d in range(1, zs)]
    peers = [near_dev(*n) for n in near] + line + [left, right]

    w = DILATION
    middle = pl.ds(w, rows)
    loads = [
        pltpu.make_async_copy(src, dst, load.at[n])
        for n, (src, dst) in enumerate(
            (
                (bottle, bx.at[middle]), (noise, nx.at[middle]), (feats, fx.at[middle]), (goal, gx),
            )
        )
    ]
    for c in loads:
        c.start()
    barrier = pltpu.get_barrier_semaphore()
    for peer in peers:
        pl.semaphore_signal(barrier, inc=1, device_id=peer, device_id_type=pl.DeviceIdType.MESH)
    blank = jnp.zeros((share, GROUP), F32)
    for g in range(groups):
        for m in range(5):
            shard = entry if m == 0 else leave if m == 4 else filters.at[m - 1]
            part = shard[:, g * GROUP:(g + 1) * GROUP].astype(F32)
            low = jnp.concatenate([part, blank], axis=0)
            high = jnp.concatenate([blank, part], axis=0)
            wpad[g, m] = jnp.where(core == 0, low, high).astype(BF16)
    pl.semaphore_wait(barrier, len(peers))

    def remote(src, dst, ssem, rsem, dev):
        c = pltpu.make_async_remote_copy(
            src_ref=src, dst_ref=dst, send_sem=ssem, recv_sem=rsem,
            device_id=dev, device_id_type=pl.DeviceIdType.MESH,
        )
        return c

    def drain(ref, sem):
        pltpu.make_async_copy(ref, ref, sem).wait()

    mine = pl.ds(core * side, side)
    theirs = pl.ds((1 - core) * side, side)
    inits = []
    for n, (first, size) in enumerate(PHASES):
        inits.append(
            remote(
                wpad.at[theirs, pl.ds(first, size)], wpeer.at[theirs, pl.ds(first, size)],
                init_send.at[n], init_recv.at[n], twin,
            )
        )
    inits.append(remote(wpad.at[mine], wpeer.at[mine], init_send.at[3], init_recv.at[3], twin))
    for c in inits:
        c.start()
    to_left = []
    to_right = []
    for n, (src, dst) in enumerate(((feats, fx), (noise, nx), (bottle, bx))):
        to_left.append(
            remote(src.at[pl.ds(0, w)], dst.at[pl.ds(w + rows, w)], halo_send.at[2 * n], halo_recv.at[2 * n], left)
        )
        to_right.append(
            remote(src.at[pl.ds(rows - w, w)], dst.at[pl.ds(0, w)], halo_send.at[2 * n + 1], halo_recv.at[2 * n + 1], right)
        )

    @pl.when(ctx > 0)
    def _():
        for c in to_left:
            c.start()

    @pl.when(ctx < count - 1)
    def _():
        for c in to_right:
            c.start()

    @pl.when(ctx == 0)
    def _():
        for dst in (fx, nx, bx):
            dst[0:w, :] = jnp.zeros((w, dst.shape[1]), BF16)

    @pl.when(ctx == count - 1)
    def _():
        for dst in (fx, nx, bx):
            dst[w + rows:, :] = jnp.zeros((w, dst.shape[1]), BF16)

    def chip_of(k):
        return lax.rem(zz + zs - k % zs, zs) * 2 + (yy if k < zs else 1 - yy)

    g_pair = core * side + par
    g_mid = core * side + 1
    g_own = core * side + 2 * par
    g_x = core * side + 2 - 2 * par

    def piece(n, g, many, k, blocks=1):
        first, size = PHASES[n]
        return weights.at[pl.ds(g, many), pl.ds(first, size), pl.ds(k * unit, blocks * unit), :]

    beside = near_dev(0, 1, 0)

    def plane_copy(n, k):
        dst = piece(n, g_pair, 2, k)
        src = piece(n, g_pair, 2, 0 if k < zs else k - zs)
        return remote(src, dst, bulk_send.at[0], ring_recv.at[n * others + k - 1], line[k - 1] if k < zs else beside)

    def to_twin(n, part, p):
        remote(p, p, bulk_send.at[2], core_recv.at[n + 2 * part if n == 1 else n], twin).start()

    def stretch(part):
        return (zs + 1, zs - 1) if part else (1, zs)

    def x_copy(n, part, g):
        p = piece(n, g, 1, *stretch(part))
        return remote(p, p, bulk_send.at[1], x_recv.at[n * 2 + part], across)

    def hop(n, part):
        first, blocks = stretch(part)
        for k in range(first, first + blocks):
            plane_copy(n, k).wait_recv()
            if k < zs:
                plane_copy(n, k + zs).start()
        x_copy(n, part, g_own).start()
        to_twin(n, part, piece(n, g_pair, 2, first, blocks))

    def xhop(n, part):
        x_copy(n, part, g_x).wait_recv()
        to_twin(n, part, piece(n, g_x, 1, *stretch(part)))

    first_half, last_half = 0, 1

    def settle(n, sem, blocks):
        first, size = PHASES[n]
        drain(weights.at[pl.ds(0, side), pl.ds(first, size), pl.ds(0, blocks * unit)], core_recv.at[sem])

    def assemble(n, begin):
        first, size = PHASES[n]
        for g in range(side):
            for m in range(first, first + size):
                weights[begin + g, m, 0:unit, :] = wpad[begin + g, m] + wpeer[begin + g, m]

    def launch(n):
        p = remote(wpad.at[mine, pl.ds(*PHASES[n])], wpeer.at[mine, pl.ds(*PHASES[n])], init_send.at[n], init_recv.at[n], twin)
        p.wait_recv()
        assemble(n, core * side)
        for k in range(1, zs + 1):
            plane_copy(n, k).start()

    launch(0)
    launch(1)
    for c in loads:
        c.wait()

    def outer(g):
        cols = pl.ds(pl.multiple_of(g * GROUP, GROUP), GROUP)
        return lax.dot_general(
            bx[middle, :], nx[middle, cols], (((0,), (0,)), ((), ())), preferred_element_type=F32
        ).reshape(chips, unit, GROUP)

    for g in range(side):
        csend[:, :, g * GROUP:(g + 1) * GROUP] = outer((1 - core) * side + g).astype(BF16)
    rs_core = remote(csend, crecv, rs_send.at[0], rs_recv.at[0], twin)
    rs_core.start()
    launch(2)
    hop(0, first_half)
    for g in range(side):
        keep[:, :, g * GROUP:(g + 1) * GROUP] = outer(core * side + g)
    hop(0, last_half)
    xhop(0, first_half)
    rs_core.wait_recv()
    for z in range(zs):
        ysend[z] = (keep[2 * z + 1 - yy] + crecv[2 * z + 1 - yy].astype(F32)).astype(BF16)
    rs_y = remote(ysend, yrecv, rs_send.at[1], rs_recv.at[1], near_dev(0, 1, 0))
    rs_y.start()
    remote(wpad.at[theirs], wpeer.at[theirs], init_send.at[3], init_recv.at[3], twin).wait_recv()
    for n in range(3):
        assemble(n, (1 - core) * side)
    xhop(0, last_half)

    @pl.when(ctx > 0)
    def _():
        for n in range(3):
            to_left[n].wait_send()
            to_right[n].wait_recv()

    @pl.when(ctx < count - 1)
    def _():
        for n in range(3):
            to_right[n].wait_send()
            to_left[n].wait_recv()

    order = lax.broadcasted_iota(jnp.int32, (bot, bot), 1)
    wanted = order
    for k in range(chips):
        wanted = jnp.where(order >= k * unit, order + (chip_of(k) - k) * unit, wanted)
    swap = jnp.where(lax.broadcasted_iota(jnp.int32, (bot, bot), 0) == wanted, 1.0, 0.0).astype(BF16)
    bo[...] = jnp.dot(bx[...], swap, preferred_element_type=F32).astype(BF16)
    settle(0, 0, others)

    edge = lax.broadcasted_iota(jnp.int32, (rows + 2 * w, 1), 0)
    inside = jnp.logical_and(
        jnp.logical_or(edge >= w, ctx > 0), jnp.logical_or(edge < w + rows, ctx < count - 1)
    )

    def enter(g):
        cols = pl.ds(g * GROUP, GROUP)
        b = fx[:, cols].astype(F32) + jnp.dot(bo[...], weights[g, 0], preferred_element_type=F32)
        off = nx[:, cols].astype(F32) * NOISE_SCALE
        base[:, cols] = b[w:w + rows]
        for p, state in enumerate((b + off, b - off)):
            act[p, :, cols] = jnp.where(inside, jax.nn.gelu(state), 0.0).astype(BF16)

    enter(0)
    enter(1)
    hop(1, first_half)
    enter(2)
    enter(3)
    rs_y.wait_recv()
    for z in range(zs):
        total = keep[2 * z + yy] + crecv[2 * z + yy].astype(F32) + yrecv[z].astype(F32)
        keep[2 * z + yy] = total
        zsend[z] = total.astype(BF16)
    rs_z = []
    for d in range(1, zs):
        c = remote(zsend.at[lax.rem(zz + d, zs)], zrecv.at[d - 1], rs_send.at[1 + d], rs_recv.at[1 + d], line[d - 1])
        c.start()
        rs_z.append(c)
    hop(2, first_half)
    xhop(1, first_half)
    enter(4)
    enter(5)
    hop(1, last_half)
    soon = (zs + 1) * unit
    settle(1, 1, zs)

    def mix(k, begin, size):
        total = jnp.zeros((2 * rows, size), F32)
        for g in range(groups):
            left_side = act[:, k * w:k * w + rows, g * GROUP:(g + 1) * GROUP].reshape(2 * rows, GROUP)
            total = total + lax.dot_general(
                left_side, weights[g, 1 + k, begin:begin + size, :],
                (((1,), (1,)), ((), ())), preferred_element_type=F32,
            )
        return total

    mixed[...] = mix(0, 0, soon)
    hop(2, last_half)
    xhop(1, last_half)
    xhop(2, first_half)
    mixed[...] += mix(1, 0, soon)
    for c in rs_z:
        c.wait_recv()
    owned = keep[chip]
    for d in range(zs - 1):
        owned = owned + zrecv[d].astype(F32)
    pair[par] = owned
    xsend[...] = owned.astype(BF16)
    rs_x = remote(xsend, xrecv, rs_send.at[1 + zs], rs_recv.at[1 + zs], across)
    rs_x.start()
    xhop(2, last_half)
    inner[...] = jax.nn.gelu(mixed[...] + mix(2, 0, soon)).astype(BF16)
    settle(1, 3, others - zs)
    mixed_late[...] = mix(0, soon, bot - soon)
    mixed_late[...] += mix(1, soon, bot - soon)
    inner_late[...] = jax.nn.gelu(mixed_late[...] + mix(2, soon, bot - soon)).astype(BF16)
    rs_x.wait_recv()
    pair[1 - par] = xrecv[...].astype(F32)
    give = pl.ds(pl.multiple_of((1 - core) * (unit // 2), 8), unit // 2)
    have = pl.ds(pl.multiple_of(core * (unit // 2), 8), unit // 2)
    rs_f = remote(pair.at[:, give, :], prow, rs_send.at[2 + zs], rs_recv.at[2 + zs], twin)
    rs_f.start()
    settle(2, 2, others)

    lanes = jnp.zeros((1, GROUP), F32)
    for g in range(groups):
        cols = pl.ds(g * GROUP, GROUP)
        off = nx[middle, cols].astype(F32) * NOISE_SCALE
        b = base[:, cols]
        outs = jnp.dot(inner[...], weights[g, 4, 0:soon, :], preferred_element_type=F32)
        outs = outs + jnp.dot(inner_late[...], weights[g, 4, soon:bot, :], preferred_element_type=F32)
        upper = b + off + outs[:rows]
        lower = b - off + outs[rows:]
        both = upper + lower
        blended[:, cols] = (both * 0.5).astype(BF16)
        lanes = lanes + jnp.sum((upper - lower) * (both - 2.0 * gx[:, cols].astype(F32)), axis=0, keepdims=True)
    local = jnp.sum(lanes, axis=1, keepdims=True) / (rows * count * chans)
    shelf = lax.broadcasted_iota(jnp.int32, (8, 128), 0)
    gaps1[0] = jnp.where(shelf == par, local, 0.0)
    sent = []
    for i, n in enumerate(near):
        c = remote(gaps1.at[0], gaps1.at[i + 1], bulk_send.at[3], bulk_send.at[4], near_dev(*n))
        c.start()
    drain(gaps1.at[pl.ds(1, len(near))], bulk_send.at[4])
    drain(gaps1.at[pl.ds(1, len(near))], bulk_send.at[3])
    gaps2[0] = jnp.sum(gaps1[...], axis=0)
    for d in range(1, zs):
        remote(gaps2.at[0], gaps2.at[d], bulk_send.at[5], bulk_send.at[6], line[d - 1]).start()
    rs_f.wait()
    drain(gaps2.at[pl.ds(1, zs - 1)], bulk_send.at[6])
    drain(gaps2.at[pl.ds(1, zs - 1)], bulk_send.at[5])
    factors = jnp.sum(gaps2[...], axis=0) / (2.0 * NOISE_SCALE)
    f0 = factors[0:1, 0:1]
    f1 = factors[1:2, 0:1]
    here = pl.ds(pl.multiple_of(core * half, 128), half)
    there = pl.ds(pl.multiple_of((1 - core) * half, 128), half)
    estimate[:, here] = f0 * pair[0, have, :] + f1 * pair[1, have, :]
    estimate[:, there] = f0 * prow[0] + f1 * prow[1]

    rs_core.wait_send()
    rs_y.wait_send()
    rs_x.wait_send()
    for c in rs_z:
        c.wait_send()
    for c in inits:
        c.wait_send()
    for n, ways in enumerate((2, 1, 3)):
        drain(weights.at[pl.ds(0, ways), :, pl.ds(0, others * unit)], bulk_send.at[n])


def fused(features, bottleneck, node_noise, targets, entry_weight, conv_filters, exit_weight):
    count = lax.axis_size("ctx")
    chips = count // 2
    _, rows, chans = features.shape
    bot = bottleneck.shape[2]
    share = entry_weight.shape[0]
    unit = 2 * share
    groups = chans // GROUP
    zs = chips // 2
    wide = rows + 2 * DILATION
    half = chans // 2
    soon = (zs + 1) * unit
    blended, estimate = pl.pallas_call(
        functools.partial(kernel, chips),
        out_shape=(
            jax.ShapeDtypeStruct((rows, chans), BF16),
            jax.ShapeDtypeStruct((share, chans), F32),
        ),
        in_specs=[pl.BlockSpec(memory_space=pltpu.HBM)] * 4 + [pl.BlockSpec(memory_space=pltpu.VMEM)] * 3,
        out_specs=[pl.BlockSpec(memory_space=pltpu.VMEM)] * 2,
        scratch_shapes=[
            pltpu.VMEM((groups, 5, bot, GROUP), BF16),
            pltpu.VMEM((groups, 5, unit, GROUP), BF16),
            pltpu.VMEM((groups, 5, unit, GROUP), BF16),
            pltpu.VMEM((wide, chans), BF16),
            pltpu.VMEM((wide, chans), BF16),
            pltpu.VMEM((wide, bot), BF16),
            pltpu.VMEM((wide, bot), BF16),
            pltpu.VMEM((rows, chans), BF16),
            pltpu.VMEM((2, wide, chans), BF16),
            pltpu.VMEM((rows, chans), F32),
            pltpu.VMEM((2 * rows, soon), F32),
            pltpu.VMEM((2 * rows, soon), BF16),
            pltpu.VMEM((2 * rows, bot - soon), F32),
            pltpu.VMEM((2 * rows, bot - soon), BF16),
            pltpu.VMEM((chips, unit, half), F32),
            pltpu.VMEM((chips, unit, half), BF16),
            pltpu.VMEM((chips, unit, half), BF16),
            pltpu.VMEM((zs, unit, half), BF16),
            pltpu.VMEM((zs, unit, half), BF16),
            pltpu.VMEM((zs, unit, half), BF16),
            pltpu.VMEM((zs - 1, unit, half), BF16),
            pltpu.VMEM((unit, half), BF16),
            pltpu.VMEM((unit, half), BF16),
            pltpu.VMEM((2, unit, half), F32),
            pltpu.VMEM((2, unit // 2, half), F32),
            pltpu.VMEM((8, 8, 128), F32),
            pltpu.VMEM((zs, 8, 128), F32),
            pltpu.SemaphoreType.DMA((3 * (chips - 1),)),
            pltpu.SemaphoreType.DMA((6,)),
            pltpu.SemaphoreType.DMA((4,)),
            pltpu.SemaphoreType.DMA((7,)),
            pltpu.SemaphoreType.DMA((4,)),
            pltpu.SemaphoreType.DMA((4,)),
            pltpu.SemaphoreType.DMA((6,)),
            pltpu.SemaphoreType.DMA((6,)),
            pltpu.SemaphoreType.DMA((3 + zs,)),
            pltpu.SemaphoreType.DMA((3 + zs,)),
            pltpu.SemaphoreType.DMA((4,)),
        ],
        compiler_params=pltpu.CompilerParams(
            collective_id=0, has_side_effects=True, vmem_limit_bytes=59 * 1024 * 1024
        ),
    )(
        features[0], bottleneck[0], node_noise[0], targets[0],
        entry_weight, jnp.swapaxes(conv_filters, 1, 2), exit_weight,
    )
    return blended[None], estimate


def solution(mesh):
    small = mesh.shape["ctx"] == 16 and mesh.shape["dp"] == 2
    return jax.shard_map(
        fused if small else body,
        mesh=mesh,
        in_specs=(
            P("dp", "ctx", None),
            P("dp", "ctx", None),
            P("dp", "ctx", None),
            P("dp", "ctx", None),
            P("ctx", None),
            P(None, None, "ctx"),
            P("ctx", None),
        ),
        out_specs=(P("dp", "ctx", None), P("ctx", None)),
        check_vma=False,
    )
```

```python
import functools

import jax
import jax.numpy as jnp
from jax import lax
from jax.experimental import pallas as pl
from jax.experimental.pallas import tpu as pltpu
from jax.sharding import PartitionSpec as P

DILATION = 32


NOISE_SCALE = 0.1


def padded_2(cells, sides, width):
    for axis, dim in sides:
        count = lax.axis_size(axis)
        ends = count - 1
        head = lax.slice_in_dim(cells, 0, width, axis=dim)
        tail = lax.slice_in_dim(cells, cells.shape[dim] - width, cells.shape[dim], axis=dim)
        cells = jnp.concatenate(
            [
                lax.ppermute(tail, axis, [(i, (i + 1) % count) for i in range(ends)]),
                cells,
                lax.ppermute(head, axis, [((i + 1) % count, i) for i in range(ends)]),
            ],
            axis=dim,
        )
    return cells


def taps_for(padded, row_count, spacing, portion):
    summed = jnp.dot(padded[..., 0:row_count, :], portion[0], preferred_element_type=jnp.float32)
    summed = summed + jnp.dot(
        padded[..., spacing : spacing + row_count, :],
        portion[1],
        preferred_element_type=jnp.float32,
    )
    summed = summed + jnp.dot(
        padded[..., 2 * spacing : 2 * spacing + row_count, :],
        portion[2],
        preferred_element_type=jnp.float32,
    )
    return summed


def rows_for(left_side, portion):
    return jnp.dot(left_side, portion, preferred_element_type=jnp.float32)


def body(features, bottleneck, node_noise, targets, entry_weight, conv_filters, exit_weight):
    feats = features[0]
    bottle = bottleneck[0]
    jitter = node_noise[0]
    goal = targets[0].astype(jnp.float32)
    row_count = feats.shape[0]
    chan_count = feats.shape[1]
    spacing = DILATION
    baseline = feats.astype(jnp.float32) + rows_for(
        bottle, lax.all_gather(entry_weight, "ctx", axis=0, tiled=True)
    )
    offset_field = jitter.astype(jnp.float32) * NOISE_SCALE
    results = []
    for polarity in (1.0, -1.0):
        state = baseline + polarity * offset_field
        activated = jax.nn.gelu(state).astype(jnp.bfloat16)
        padded = padded_2(activated, (("ctx", 0),), spacing)
        mixed = taps_for(
            padded, row_count, spacing, lax.all_gather(conv_filters, "ctx", axis=2, tiled=True)
        )
        inner = jax.nn.gelu(mixed).astype(jnp.bfloat16)
        results.append(
            state + rows_for(inner, lax.all_gather(exit_weight, "ctx", axis=0, tiled=True))
        )
    upper = results[0]
    lower = results[1]
    blended = ((upper + lower) * 0.5).astype(jnp.bfloat16)[None]
    local_gap = jnp.sum((upper - lower) * (upper + lower - 2.0 * goal)) / (
        row_count * lax.axis_size("ctx") * chan_count
    )
    factor = lax.psum(local_gap, "ctx") / (2.0 * NOISE_SCALE)
    local_term = factor * lax.dot_general(
        bottle, jitter, (((0,), (0,)), ((), ())), preferred_element_type=jnp.float32
    )
    grouped = lax.psum(local_term, "dp")
    estimate = lax.psum_scatter(grouped, "ctx", scatter_dimension=0, tiled=True)
    return (blended, estimate)


F32 = jnp.float32
BF16 = jnp.bfloat16
GROUP = 256
PHASES = ((0, 1), (1, 3), (4, 1))
HOPS = 4
EARLY = 2


def chip_at(position, chips):
    return jnp.where(position < chips // 2, 2 * position, 2 * (chips - 1 - position) + 1)


def kernel(
    chips,
    feats, bottle, noise, goal, entry, filters, leave,
    blended, estimate,
    weights, wpad, wpeer, fx, nx, bx, bo, gx, act, base, mixed, inner, mixed_late, inner_late,
    keep, csend, crecv, ysend, yrecv, zsend, zrecv, xsend, xrecv, pair, prow, gaps1, gaps2,
    ring_recv, x_recv, core_recv, bulk_send, init_send, init_recv, halo_send, halo_recv, rs_send, rs_recv, load,
):
    rows, chans = feats.shape
    bot = bottle.shape[1]
    share = entry.shape[0]
    unit = 2 * share
    half = chans // 2
    groups = chans // GROUP
    side = groups // 2
    zs = chips // 2
    others = chips - 1
    dp = lax.axis_index("dp")
    ctx = lax.axis_index("ctx")
    count = 2 * chips
    core = lax.rem(ctx, 2)
    chip = ctx // 2
    yy = lax.rem(chip, 2)
    zz = chip // 2
    par = lax.rem(dp, 2)
    mate = dp + 1 - 2 * par
    place = jnp.where(yy == 0, zz, chips - 1 - zz)

    def at(d, z, y, c):
        return {"dp": d, "ctx": (z * 2 + y) * 2 + c}

    def on_ring(p):
        return lax.rem(p + chips, chips)

    twin = at(dp, zz, yy, 1 - core)
    across = at(mate, zz, yy, core)
    near = [(i, j, k) for i in range(2) for j in range(2) for k in range(2) if i or j or k]

    def near_dev(i, j, k):
        return at(
            mate if i else dp,
            zz,
            1 - yy if j else yy,
            1 - core if k else core,
        )

    left = {"dp": dp, "ctx": lax.rem(ctx + count - 1, count)}
    right = {"dp": dp, "ctx": lax.rem(ctx + 1, count)}
    line = [at(dp, lax.rem(zz + d, zs), yy, core) for d in range(1, zs)]
    peers = [near_dev(*n) for n in near] + line + [left, right]

    w = DILATION
    middle = pl.ds(w, rows)
    loads = [
        pltpu.make_async_copy(src, dst, load.at[n])
        for n, (src, dst) in enumerate(
            (
                (bottle, bx.at[middle]), (noise, nx.at[middle]), (feats, fx.at[middle]), (goal, gx),
            )
        )
    ]
    for c in loads:
        c.start()
    blank = jnp.zeros((share, GROUP), F32)
    for g in range(groups):
        for m in range(5):
            shard = entry if m == 0 else leave if m == 4 else filters.at[m - 1]
            part = shard[:, g * GROUP:(g + 1) * GROUP].astype(F32)
            low = jnp.concatenate([part, blank], axis=0)
            high = jnp.concatenate([blank, part], axis=0)
            wpad[g, m] = jnp.where(core == 0, low, high).astype(BF16)

    barrier = pltpu.get_barrier_semaphore()
    for peer in peers:
        pl.semaphore_signal(barrier, inc=1, device_id=peer, device_id_type=pl.DeviceIdType.MESH)
    pl.semaphore_wait(barrier, len(peers))

    def remote(src, dst, ssem, rsem, dev):
        c = pltpu.make_async_remote_copy(
            src_ref=src, dst_ref=dst, send_sem=ssem, recv_sem=rsem,
            device_id=dev, device_id_type=pl.DeviceIdType.MESH,
        )
        return c

    def drain(ref, sem):
        pltpu.make_async_copy(ref, ref, sem).wait()

    mine = pl.ds(core * side, side)
    theirs = pl.ds((1 - core) * side, side)
    inits = []
    for n, (first, size) in enumerate(PHASES):
        inits.append(
            remote(
                wpad.at[theirs, pl.ds(first, size)], wpeer.at[theirs, pl.ds(first, size)],
                init_send.at[n], init_recv.at[n], twin,
            )
        )
    inits.append(remote(wpad.at[mine], wpeer.at[mine], init_send.at[3], init_recv.at[3], twin))
    for c in inits:
        c.start()
    to_left = []
    to_right = []
    for n, (src, dst) in enumerate(((feats, fx), (noise, nx), (bottle, bx))):
        to_left.append(
            remote(src.at[pl.ds(0, w)], dst.at[pl.ds(w + rows, w)], halo_send.at[2 * n], halo_recv.at[2 * n], left)
        )
        to_right.append(
            remote(src.at[pl.ds(rows - w, w)], dst.at[pl.ds(0, w)], halo_send.at[2 * n + 1], halo_recv.at[2 * n + 1], right)
        )

    @pl.when(ctx > 0)
    def _():
        for c in to_left:
            c.start()

    @pl.when(ctx < count - 1)
    def _():
        for c in to_right:
            c.start()

    @pl.when(ctx == 0)
    def _():
        for dst in (fx, nx, bx):
            dst[0:w, :] = jnp.zeros((w, dst.shape[1]), BF16)

    @pl.when(ctx == count - 1)
    def _():
        for dst in (fx, nx, bx):
            dst[w + rows:, :] = jnp.zeros((w, dst.shape[1]), BF16)

    def span(d, h):
        return pl.ds(unit * (0 if h == 0 else min(2 * h - 1 + d, chips - 1)), unit)

    def chip_of(k):
        return chip_at(on_ring(place if k == 0 else place - (k + 1) // 2 if k % 2 else place + k // 2), chips)

    g_pair = core * side + par
    g_mid = core * side + 1
    g_own = core * side + 2 * par
    g_x = core * side + 2 - 2 * par

    def piece(n, g, many, d, h):
        first, size = PHASES[n]
        return weights.at[pl.ds(g, many), pl.ds(first, size), span(d, h), :]

    def ring_piece(n, d, h, start):
        if h < HOPS:
            return piece(n, g_pair, 2, d, start)
        return piece(n, g_mid if d == 0 else g_own, 1, d, start)

    def toward(d):
        q = chip_at(on_ring(place + 1 if d == 0 else place - 1), chips)
        return {"dp": dp, "ctx": q * 2 + core}

    nexts = (toward(0), toward(1))

    def ring_copy(n, d, h):
        return remote(ring_piece(n, d, h, h - 1), ring_piece(n, d, h, h), bulk_send.at[0], ring_recv.at[n * 2 * HOPS + 2 * (h - 1) + d], nexts[d])

    def to_twin(n, h, p):
        late = 1 if n == 1 and h > EARLY else 0
        remote(p, p, bulk_send.at[2], core_recv.at[n + 2 * late], twin).start()

    def x_copy(n, d, h, g):
        p = piece(n, g, 1, d, h)
        return remote(p, p, bulk_send.at[1], x_recv.at[n * 2 * HOPS + 2 * (h - 1) + d], across)

    def hop(n, h):
        for d in range(2):
            ring_copy(n, d, h).wait_recv()
            if h < HOPS:
                ring_copy(n, d, h + 1).start()
            if h < HOPS or d == 1:
                x_copy(n, d, h, g_own).start()
        for d in range(2):
            to_twin(n, h, ring_piece(n, d, h, h))

    def xhop(n, h):
        for d in range(2):
            if h < HOPS or d == 1:
                x_copy(n, d, h, g_x).wait_recv()
                to_twin(n, h, piece(n, g_x, 1, d, h))

    def settle(n, sem, blocks):
        first, size = PHASES[n]
        drain(weights.at[pl.ds(0, side), pl.ds(first, size), pl.ds(0, blocks * unit)], core_recv.at[sem])

    def assemble(n, begin):
        first, size = PHASES[n]
        for g in range(side):
            for m in range(first, first + size):
                weights[begin + g, m, 0:unit, :] = wpad[begin + g, m] + wpeer[begin + g, m]

    def launch(n):
        p = remote(wpad.at[mine, pl.ds(*PHASES[n])], wpeer.at[mine, pl.ds(*PHASES[n])], init_send.at[n], init_recv.at[n], twin)
        p.wait_recv()
        assemble(n, core * side)
        for d in range(2):
            ring_copy(n, d, 1).start()

    launch(0)
    launch(1)
    for c in loads:
        c.wait()

    def outer(side_of):
        cols = pl.ds(pl.multiple_of(side_of * half, 128), half)
        return lax.dot_general(
            bx[middle, :], nx[middle, cols], (((0,), (0,)), ((), ())), preferred_element_type=F32
        ).reshape(chips, unit, half)

    csend[...] = outer(1 - core).astype(BF16)
    rs_core = remote(csend, crecv, rs_send.at[0], rs_recv.at[0], twin)
    rs_core.start()
    hop(0, 1)
    launch(2)
    keep[...] = outer(core)
    hop(0, 2)
    xhop(0, 1)
    hop(1, 1)
    rs_core.wait_recv()
    for z in range(zs):
        ysend[z] = (keep[2 * z + 1 - yy] + crecv[2 * z + 1 - yy].astype(F32)).astype(BF16)
    rs_y = remote(ysend, yrecv, rs_send.at[1], rs_recv.at[1], near_dev(0, 1, 0))
    rs_y.start()
    hop(0, 3)
    xhop(0, 2)
    remote(wpad.at[theirs], wpeer.at[theirs], init_send.at[3], init_recv.at[3], twin).wait_recv()
    for n in range(3):
        assemble(n, (1 - core) * side)
    hop(0, 4)
    xhop(0, 3)
    hop(1, 2)
    xhop(0, 4)
    xhop(1, 1)
    hop(2, 1)
    rs_y.wait_recv()
    for z in range(zs):
        total = keep[2 * z + yy] + crecv[2 * z + yy].astype(F32) + yrecv[z].astype(F32)
        keep[2 * z + yy] = total
        zsend[z] = total.astype(BF16)
    rs_z = []
    for d in range(1, zs):
        c = remote(zsend.at[lax.rem(zz + d, zs)], zrecv.at[d - 1], rs_send.at[1 + d], rs_recv.at[1 + d], line[d - 1])
        c.start()
        rs_z.append(c)

    @pl.when(ctx > 0)
    def _():
        for n in range(3):
            to_left[n].wait_send()
            to_right[n].wait_recv()

    @pl.when(ctx < count - 1)
    def _():
        for n in range(3):
            to_right[n].wait_send()
            to_left[n].wait_recv()

    order = lax.broadcasted_iota(jnp.int32, (bot, bot), 1)
    wanted = order
    for k in range(chips):
        wanted = jnp.where(order >= k * unit, order + (chip_of(k) - k) * unit, wanted)
    swap = jnp.where(lax.broadcasted_iota(jnp.int32, (bot, bot), 0) == wanted, 1.0, 0.0).astype(BF16)
    bo[...] = jnp.dot(bx[...], swap, preferred_element_type=F32).astype(BF16)
    settle(0, 0, others)

    edge = lax.broadcasted_iota(jnp.int32, (rows + 2 * w, 1), 0)
    inside = jnp.logical_and(
        jnp.logical_or(edge >= w, ctx > 0), jnp.logical_or(edge < w + rows, ctx < count - 1)
    )

    def enter(g):
        cols = pl.ds(g * GROUP, GROUP)
        b = fx[:, cols].astype(F32) + jnp.dot(bo[...], weights[g, 0], preferred_element_type=F32)
        off = nx[:, cols].astype(F32) * NOISE_SCALE
        base[:, cols] = b[w:w + rows]
        for p, state in enumerate((b + off, b - off)):
            act[p, :, cols] = jnp.where(inside, jax.nn.gelu(state), 0.0).astype(BF16)

    enter(0)
    hop(1, 3)
    xhop(1, 2)
    enter(1)
    hop(2, 2)
    xhop(2, 1)
    enter(2)
    enter(3)
    hop(1, 4)
    xhop(1, 3)
    enter(4)
    enter(5)
    hop(2, 3)
    xhop(1, 4)
    xhop(2, 2)
    soon = (2 * EARLY + 1) * unit
    settle(1, 1, 2 * EARLY)

    def mix(k, begin, size):
        total = jnp.zeros((2 * rows, size), F32)
        for g in range(groups):
            left_side = act[:, k * w:k * w + rows, g * GROUP:(g + 1) * GROUP].reshape(2 * rows, GROUP)
            total = total + lax.dot_general(
                left_side, weights[g, 1 + k, begin:begin + size, :],
                (((1,), (1,)), ((), ())), preferred_element_type=F32,
            )
        return total

    mixed[...] = mix(0, 0, soon)
    hop(2, 4)
    xhop(2, 3)
    mixed[...] += mix(1, 0, soon)
    for c in rs_z:
        c.wait_recv()
    owned = keep[chip]
    for d in range(zs - 1):
        owned = owned + zrecv[d].astype(F32)
    pair[par] = owned
    xsend[...] = owned.astype(BF16)
    rs_x = remote(xsend, xrecv, rs_send.at[1 + zs], rs_recv.at[1 + zs], across)
    rs_x.start()
    xhop(2, 4)
    inner[...] = jax.nn.gelu(mixed[...] + mix(2, 0, soon)).astype(BF16)
    settle(1, 3, others - 2 * EARLY)
    mixed_late[...] = mix(0, soon, bot - soon)
    mixed_late[...] += mix(1, soon, bot - soon)
    inner_late[...] = jax.nn.gelu(mixed_late[...] + mix(2, soon, bot - soon)).astype(BF16)
    rs_x.wait_recv()
    pair[1 - par] = xrecv[...].astype(F32)
    give = pl.ds(pl.multiple_of((1 - core) * (unit // 2), 8), unit // 2)
    have = pl.ds(pl.multiple_of(core * (unit // 2), 8), unit // 2)
    rs_f = remote(pair.at[:, give, :], prow, rs_send.at[2 + zs], rs_recv.at[2 + zs], twin)
    rs_f.start()
    settle(2, 2, others)

    lanes = jnp.zeros((1, GROUP), F32)
    for g in range(groups):
        cols = pl.ds(g * GROUP, GROUP)
        off = nx[middle, cols].astype(F32) * NOISE_SCALE
        b = base[:, cols]
        outs = jnp.dot(inner[...], weights[g, 4, 0:soon, :], preferred_element_type=F32)
        outs = outs + jnp.dot(inner_late[...], weights[g, 4, soon:bot, :], preferred_element_type=F32)
        upper = b + off + outs[:rows]
        lower = b - off + outs[rows:]
        both = upper + lower
        blended[:, cols] = (both * 0.5).astype(BF16)
        lanes = lanes + jnp.sum((upper - lower) * (both - 2.0 * gx[:, cols].astype(F32)), axis=0, keepdims=True)
    local = jnp.sum(lanes, axis=1, keepdims=True) / (rows * count * chans)
    shelf = lax.broadcasted_iota(jnp.int32, (8, 128), 0)
    gaps1[0] = jnp.where(shelf == par, local, 0.0)
    sent = []
    for i, n in enumerate(near):
        c = remote(gaps1.at[0], gaps1.at[i + 1], bulk_send.at[3], bulk_send.at[4], near_dev(*n))
        c.start()
    drain(gaps1.at[pl.ds(1, len(near))], bulk_send.at[4])
    drain(gaps1.at[pl.ds(1, len(near))], bulk_send.at[3])
    gaps2[0] = jnp.sum(gaps1[...], axis=0)
    for d in range(1, zs):
        remote(gaps2.at[0], gaps2.at[d], bulk_send.at[5], bulk_send.at[6], line[d - 1]).start()
    rs_f.wait()
    drain(gaps2.at[pl.ds(1, zs - 1)], bulk_send.at[6])
    drain(gaps2.at[pl.ds(1, zs - 1)], bulk_send.at[5])
    factors = jnp.sum(gaps2[...], axis=0) / (2.0 * NOISE_SCALE)
    f0 = factors[0:1, 0:1]
    f1 = factors[1:2, 0:1]
    here = pl.ds(pl.multiple_of(core * half, 128), half)
    there = pl.ds(pl.multiple_of((1 - core) * half, 128), half)
    estimate[:, here] = f0 * pair[0, have, :] + f1 * pair[1, have, :]
    estimate[:, there] = f0 * prow[0] + f1 * prow[1]

    rs_core.wait_send()
    rs_y.wait_send()
    rs_x.wait_send()
    for c in rs_z:
        c.wait_send()
    for c in inits:
        c.wait_send()
    for n, ways in enumerate((2, 1, 3)):
        drain(weights.at[pl.ds(0, ways), :, pl.ds(0, others * unit)], bulk_send.at[n])


def fused(features, bottleneck, node_noise, targets, entry_weight, conv_filters, exit_weight):
    count = lax.axis_size("ctx")
    chips = count // 2
    _, rows, chans = features.shape
    bot = bottleneck.shape[2]
    share = entry_weight.shape[0]
    unit = 2 * share
    groups = chans // GROUP
    zs = chips // 2
    wide = rows + 2 * DILATION
    half = chans // 2
    soon = (2 * EARLY + 1) * unit
    blended, estimate = pl.pallas_call(
        functools.partial(kernel, chips),
        out_shape=(
            jax.ShapeDtypeStruct((rows, chans), BF16),
            jax.ShapeDtypeStruct((share, chans), F32),
        ),
        in_specs=[pl.BlockSpec(memory_space=pltpu.HBM)] * 4 + [pl.BlockSpec(memory_space=pltpu.VMEM)] * 3,
        out_specs=[pl.BlockSpec(memory_space=pltpu.VMEM)] * 2,
        scratch_shapes=[
            pltpu.VMEM((groups, 5, bot, GROUP), BF16),
            pltpu.VMEM((groups, 5, unit, GROUP), BF16),
            pltpu.VMEM((groups, 5, unit, GROUP), BF16),
            pltpu.VMEM((wide, chans), BF16),
            pltpu.VMEM((wide, chans), BF16),
            pltpu.VMEM((wide, bot), BF16),
            pltpu.VMEM((wide, bot), BF16),
            pltpu.VMEM((rows, chans), BF16),
            pltpu.VMEM((2, wide, chans), BF16),
            pltpu.VMEM((rows, chans), F32),
            pltpu.VMEM((2 * rows, soon), F32),
            pltpu.VMEM((2 * rows, soon), BF16),
            pltpu.VMEM((2 * rows, bot - soon), F32),
            pltpu.VMEM((2 * rows, bot - soon), BF16),
            pltpu.VMEM((chips, unit, half), F32),
            pltpu.VMEM((chips, unit, half), BF16),
            pltpu.VMEM((chips, unit, half), BF16),
            pltpu.VMEM((zs, unit, half), BF16),
            pltpu.VMEM((zs, unit, half), BF16),
            pltpu.VMEM((zs, unit, half), BF16),
            pltpu.VMEM((zs - 1, unit, half), BF16),
            pltpu.VMEM((unit, half), BF16),
            pltpu.VMEM((unit, half), BF16),
            pltpu.VMEM((2, unit, half), F32),
            pltpu.VMEM((2, unit // 2, half), F32),
            pltpu.VMEM((8, 8, 128), F32),
            pltpu.VMEM((zs, 8, 128), F32),
            pltpu.SemaphoreType.DMA((3 * 2 * HOPS,)),
            pltpu.SemaphoreType.DMA((3 * 2 * HOPS,)),
            pltpu.SemaphoreType.DMA((4,)),
            pltpu.SemaphoreType.DMA((7,)),
            pltpu.SemaphoreType.DMA((4,)),
            pltpu.SemaphoreType.DMA((4,)),
            pltpu.SemaphoreType.DMA((6,)),
            pltpu.SemaphoreType.DMA((6,)),
            pltpu.SemaphoreType.DMA((3 + zs,)),
            pltpu.SemaphoreType.DMA((3 + zs,)),
            pltpu.SemaphoreType.DMA((4,)),
        ],
        compiler_params=pltpu.CompilerParams(
            collective_id=0, has_side_effects=True, vmem_limit_bytes=59 * 1024 * 1024
        ),
    )(
        features[0], bottleneck[0], node_noise[0], targets[0],
        entry_weight, jnp.swapaxes(conv_filters, 1, 2), exit_weight,
    )
    return blended[None], estimate


def solution(mesh):
    small = mesh.shape["ctx"] == 16 and mesh.shape["dp"] == 2
    return jax.shard_map(
        fused if small else body,
        mesh=mesh,
        in_specs=(
            P("dp", "ctx", None),
            P("dp", "ctx", None),
            P("dp", "ctx", None),
            P("dp", "ctx", None),
            P("ctx", None),
            P(None, None, "ctx"),
            P("ctx", None),
        ),
        out_specs=(P("dp", "ctx", None), P("ctx", None)),
        check_vma=False,
    )
```
